32 devices in a mesh: groups: 2 (over x), wide: 16 (over z, y, core).
Axes of the slice: x: 2, y: 2, z: 4, core: 2. Of those that a mesh axis runs over, the one named last changes fastest.
Arguments:
- tokens: bfloat16 [64, 384, 768], P(('groups', 'wide')), parts along dimension 0, may hold values from -6 to 6
- item_lengths: int32 [64, 64], P(('groups', 'wide')), parts along dimension 0, may hold values from 1 to 16, 384 in all within a row
- w_query: bfloat16 [768, 768], replicated
- w_key: bfloat16 [768, 768], replicated, may hold values from -0.21875 to 0.21875
- w_value: bfloat16 [768, 768], replicated, may hold values from -0.21875 to 0.21875
- w_output: bfloat16 [768, 768], replicated, may hold values from -0.21875 to 0.21875
- w_input: bfloat16 [3072, 768], P('wide'), may hold values from -0.21875 to 0.21875
- w_down: bfloat16 [3072, 768], P('wide'), may hold values from -0.109375 to 0.109375
- norm_attn: float32 [768], replicated, may hold values from 0.1 to 1.9
- norm_ffn: float32 [768], replicated, may hold values from 0.1 to 1.9
- norm_final: float32 [768], replicated, may hold values from 0.1 to 1.9
- owner: int32 [4096, 1], P(('groups', 'wide')), parts along dimension 0, may hold values from 0 to 15; in each aligned block of 128 rows (0 to 127, 128 to 255, ...) at most 16 rows name the same one
- cluster_slot: int32 [4096], P(('groups', 'wide')), parts along dimension 0, may hold values from 0 to 7
- coarse: bfloat16 [128, 768], P('wide'), may hold values from -4 to 4
- centroids: bfloat16 [128, 256, 768], P('wide'), may hold values from -0.21875 to 0.21875
Outputs:
- item_embed: bfloat16 [4096, 768], P(('groups', 'wide')), parts along dimension 0
- item_codes: float32 [4096, 256], P(('groups', 'wide')), parts along dimension 0
The draws below stay inside these ranges and needn't reach their ends.
There are 2 independent parts, one for each index of `groups`. The reference program is written for one: setup_inputs(seed, part) draws one part's arguments, and reference() takes and returns one part's arrays. A program takes and returns all parts, laid end to end along the dimension named above; an argument that names none is the same for every part. Nothing has to cross between parts.
Inputs may be any that keep to these rules, and one draw needn't show every extreme that they name: In each device's 128 rows no owner is named more than 16 times, a bound that some block reaches. `item_lengths`: each pack's lengths sum to 384; some item has exactly 16 tokens.
All inputs are finite; a program needn't handle non-finite values.
Results may differ from the reference program's by a relative error of at most 0.012.
The reference program's roundings to bfloat16 on the way (of `normed`, `query`, `probs`, `context`, `stream` and `hidden`) count: a program that leaves them out, or rounds other values in their place, can miss the bound.
Values may be sent and summed in bfloat16 or wider, within the bound.
No kernel may reach another device: no remote copies, remote signals or barrier semaphores. Data moves between devices by JAX's collectives and lax.ppermute only.
A program may use at most 128 MiB of HBM per device.

```python
import math
import jax
import jax.numpy as jnp
import numpy as np
from jax import lax

D = 768
FF = 3072
HEADS = 12
HEAD = 64
PACK_LEN = 384
ITEMS_PACK = 64
MOST = 16
CL_DEV = 8
CODES = 256
PACKS = 32
ITEMS_DEV = 128
ITEMS = 2048
CLUSTERS = 128
CAP = 16
N_WIDE = 16


def draw_w_query(key, part):
    key = jax.random.fold_in(key, 7)
    values = jax.random.normal(key, (D, D), jnp.float32) * D ** (-0.5)
    return values.astype(jnp.bfloat16)


def with_ends(values, rng, smallest, high):
    dims = values.shape
    spot = [jax.random.randint(jax.random.fold_in(rng, axis), (), 0, dims[axis]) for axis in range(len(dims))]
    values = values.at[tuple(spot)].set(smallest)
    longest = dims.index(max(dims))
    spot[longest] = (spot[longest] + 1) % dims[longest]
    return values.at[tuple(spot)].set(high)


def block_levels(own_key, dims, shards, smallest, largest):
    def one(position, shards_of):
        heights = jax.random.uniform(jax.random.fold_in(jax.random.fold_in(own_key, 6), position), (shards_of,), jnp.float32, smallest / len(shards), largest / len(shards))
        return jnp.repeat(jnp.exp(heights), dims[position] // shards_of).reshape((-1,) + (1,) * (len(dims) - position - 1))

    loudness = one(*shards[0])
    for cut in shards[1:]:
        loudness = loudness * one(*cut)
    return loudness


def split_up(count, total, bound, lean):
    loads = [(1 << 20) // math.isqrt(grade ** lean) + 1 for grade in range(2, count + 1)]
    spare, given = total - bound - (count - 1), [1] * (count - 1)
    while spare > 0:
        movable = [i for i in range(count - 1) if given[i] < bound]
        pool, remaining = sum([loads[i] for i in movable]), spare
        for i in movable:
            extra = min(bound - given[i], max(1, remaining * loads[i] // pool), spare)
            given[i] = given[i] + extra
            spare = spare - extra
    return np.array([bound] + given)


def ragged_sizes(stream_key, count, total, reach, slope):
    if count == 2:
        one = jax.random.randint(stream_key, (), max(1, total - reach), min(reach, total - 1) + 1)
        return jnp.stack([one, total - one])
    tallies = jnp.asarray(split_up(count, total, reach, slope), jnp.int32)
    couples = (count - 1) // 2
    source_of, taker = tallies[1:1 + 2 * couples:2], tallies[2:2 + 2 * couples:2]
    margin = jnp.minimum(source_of - 1, reach - taker)
    moved = jax.random.randint(jax.random.fold_in(stream_key, 1), (couples,), 0, 1 << 20) % (margin + 1)
    tallies = tallies.at[1:1 + 2 * couples:2].set(source_of - moved).at[2:2 + 2 * couples:2].set(taker + moved)
    return tallies[jax.random.permutation(jax.random.fold_in(stream_key, 2), count)]


def routed_block(stream_key, own, number, rows, amount, top, most, lean):
    sequence = jax.random.permutation(stream_key, amount)
    heavy_load, usual = portions_of(amount, rows * top, most, lean, True), portions_of(amount, rows * top, most, lean, False)
    places = jnp.arange(amount)

    def named(sizes, offset_by):
        used = int((sizes > 0).sum())
        fixed = max(1, used // 4)
        moved = fixed + (places - fixed + offset_by * (used - fixed)) % max(1, amount - fixed)
        return jnp.zeros((amount,), jnp.int32).at[sequence[jnp.where(places < fixed, places, moved)]].set(jnp.asarray(sizes, jnp.int32))

    sizes = jnp.where(number % 4 == 0, named(heavy_load, number // 4), named(usual, number - number // 4 - 1))
    mixed = jax.random.permutation(jax.random.fold_in(own, 3), amount)
    source_of, taker = mixed[0:amount // 2 * 2:2], mixed[1:amount // 2 * 2:2]
    margin = jnp.minimum(sizes[source_of] - 1, most - sizes[taker]) // 2
    margin = jnp.where((source_of == sequence[0]) | (taker == sequence[0]) | (sizes[taker] == 0), 0, jnp.maximum(margin, 0))
    moved = jax.random.randint(jax.random.fold_in(own, 4), (amount // 2,), 0, 1 << 20) % (margin + 1)
    sizes = sizes.at[source_of].add(-moved).at[taker].add(moved)
    items = jnp.searchsorted(jnp.cumsum(sizes), jnp.arange(rows * top), side="right").astype(jnp.int32)
    table = items.reshape(top, rows).T
    table = table[jax.random.permutation(jax.random.fold_in(own, 1), rows)]
    offset_by = jax.random.randint(jax.random.fold_in(own, 2), (rows, 1), 0, top)
    return jnp.take_along_axis(table, (jnp.arange(top)[None, :] + offset_by) % top, axis=1)


def portions_of(count, total, bound, lean, full):
    loads = [(1 << 20) // math.isqrt(rank ** lean) + 1 for rank in range(1, count + 1)]
    largest = bound if full else min(bound, max(-(-total // count), total * loads[0] // sum(loads)))
    least = 1 if total - largest >= count - 1 else 0
    given, rest = [largest] + [least] * (count - 1), total - largest - least * (count - 1)
    while rest > 0:
        movable = [i for i in range(1, count) if given[i] < largest] or [i for i in range(1, count) if given[i] < bound]
        whole, budget = sum([loads[i] for i in movable]), rest
        for i in movable:
            addition = min(bound - given[i], max(1, budget * loads[i] // whole), rest)
            given[i] = given[i] + addition
            rest = rest - addition
    return np.array(given)


def centred(own_key, shape, deviation, reach, cuts=(), kind=jnp.bfloat16):
    level = block_levels(own_key, shape, cuts, -0.22, 0.18) if cuts else 1.0
    array = jax.random.normal(own_key, shape, jnp.float32) * deviation * level
    return jnp.minimum(jnp.maximum(array, -reach), reach).astype(kind)


def setup_inputs(seed: int = 0, part: int = 0) -> dict:
    seeds = jax.random.split(jax.random.key(seed), 16)
    part_keys = jax.random.split(jax.random.fold_in(seeds[15], part), 16)
    tokens = centred(part_keys[0], (PACKS, PACK_LEN, D), 1.0, 6.0, ((0, 16),))
    item_lengths = jax.vmap(lambda own: ragged_sizes(own, ITEMS_PACK, PACK_LEN, MOST, 1))(jax.random.split(part_keys[1], PACKS)).reshape((PACKS, ITEMS_PACK)).astype(jnp.int32)
    w_query = draw_w_query(jax.random.fold_in(seeds[15], 71), part)
    w_key = centred(seeds[3], (D, D), D ** -0.5, 0.21875)
    w_value = centred(seeds[4], (D, D), D ** -0.5, 0.21875)
    w_output = centred(seeds[5], (D, D), D ** -0.5, 0.21875)
    w_input = centred(seeds[6], (FF, D), D ** -0.5, 0.21875, ((0, 16),))
    w_down = centred(seeds[7], (FF, D), FF ** -0.5, 0.109375, ((0, 16),))
    norm_attn = jnp.clip(1.0 + 0.18 * jax.random.normal(seeds[8], (D,), jnp.float32), 0.1, 1.9)
    norm_ffn = jnp.clip(1.0 + 0.18 * jax.random.normal(seeds[9], (D,), jnp.float32), 0.1, 1.9)
    norm_final = jnp.clip(1.0 + 0.18 * jax.random.normal(seeds[10], (D,), jnp.float32), 0.1, 1.9)
    owner_keys = jax.random.split(jax.random.fold_in(part_keys[11], 1), ITEMS // ITEMS_DEV)
    owner_turns = jax.random.permutation(jax.random.fold_in(part_keys[11], 3), ITEMS // ITEMS_DEV)
    owner = jax.vmap(lambda own, number: routed_block(jax.random.fold_in(part_keys[11], 2), own, number, ITEMS_DEV, N_WIDE, 1, CAP, 2))(owner_keys, owner_turns).reshape((ITEMS, 1))
    cluster_slot = with_ends(jax.random.randint(part_keys[12], (ITEMS,), 0, CL_DEV), jax.random.fold_in(part_keys[12], 1), 0, CL_DEV - 1).astype(jnp.int32)
    coarse = centred(seeds[13], (CLUSTERS, D), 0.5, 4.0, ((0, 16),))
    centroids = centred(seeds[14], (CLUSTERS, CODES, D), D ** -0.5, 0.21875, ((0, 16),))
    return dict(tokens=tokens, item_lengths=item_lengths, w_query=w_query, w_key=w_key, w_value=w_value, w_output=w_output, w_input=w_input, w_down=w_down, norm_attn=norm_attn, norm_ffn=norm_ffn, norm_final=norm_final, owner=owner, cluster_slot=cluster_slot, coarse=coarse, centroids=centroids)


def rms(values, gain):
    mean_sq = lax.optimization_barrier(jnp.mean(values * values, axis=-1, keepdims=True))
    return values * lax.rsqrt(mean_sq + 1e-06) * gain

def encode_pack(pack, lengths, w_query, w_key, w_value, w_output, w_input, w_down, norm_attn, norm_ffn, norm_final):
    seq = pack.shape[0]
    ends = jnp.cumsum(lengths)
    places = jnp.arange(seq, dtype=jnp.int32)
    item = lax.optimization_barrier(jnp.sum((ends[None, :] <= places[:, None]).astype(jnp.int32), axis=1))
    same = item[:, None] == item[None, :]
    stream0 = pack.astype(jnp.float32)
    normed = rms(stream0, norm_attn).astype(jnp.bfloat16)
    query = jnp.dot(normed, w_query, preferred_element_type=jnp.float32).astype(jnp.bfloat16).reshape(seq, HEADS, HEAD)
    keys = jnp.dot(normed, w_key, preferred_element_type=jnp.float32).astype(jnp.bfloat16).reshape(seq, HEADS, HEAD)
    values = jnp.dot(normed, w_value, preferred_element_type=jnp.float32).astype(jnp.bfloat16).reshape(seq, HEADS, HEAD)
    scores = jnp.einsum('qhe,khe->hqk', query.astype(jnp.float32), keys.astype(jnp.float32))
    scores = jnp.where(same[None], scores, -1e+30)
    top = lax.optimization_barrier(jnp.max(scores, axis=-1, keepdims=True))
    expo = jnp.exp(scores - top)
    probs = (expo / lax.optimization_barrier(jnp.sum(expo, axis=-1, keepdims=True))).astype(jnp.bfloat16)
    context = jnp.einsum('hqk,khe->qhe', probs.astype(jnp.float32), values.astype(jnp.float32)).astype(jnp.bfloat16).reshape(seq, D)
    stream = (stream0 + jnp.dot(context, w_output, preferred_element_type=jnp.float32)).astype(jnp.bfloat16)
    normed2 = rms(stream.astype(jnp.float32), norm_ffn).astype(jnp.bfloat16)
    hidden = jax.nn.relu(jnp.dot(normed2, w_input.T, preferred_element_type=jnp.float32)).astype(jnp.bfloat16)
    final = stream.astype(jnp.float32) + jnp.dot(hidden, w_down, preferred_element_type=jnp.float32)
    select = (item[None, :] == jnp.arange(ITEMS_PACK, dtype=jnp.int32)[:, None]).astype(jnp.float32)
    pooled = jnp.dot(select, final, precision=lax.Precision.HIGHEST)
    return rms(pooled, norm_final).astype(jnp.bfloat16)

def reference(tokens, item_lengths, w_query, w_key, w_value, w_output, w_input, w_down, norm_attn, norm_ffn, norm_final, owner, cluster_slot, coarse, centroids):

    def one_pack(pair):
        return encode_pack(pair[0], pair[1], w_query, w_key, w_value, w_output, w_input, w_down, norm_attn, norm_ffn, norm_final)
    embeds = lax.map(one_pack, (tokens, item_lengths))
    clusters = (owner[:, 0] * CL_DEV + cluster_slot).astype(jnp.int32).reshape(PACKS, ITEMS_PACK)

    def one_block(pair):
        block_embed, block_cluster = pair
        books = centroids[block_cluster].astype(jnp.float32)
        centers = coarse[block_cluster].astype(jnp.float32)
        direct = jnp.einsum('id,ijd->ij', block_embed.astype(jnp.float32), books)
        offset = jnp.einsum('id,ijd->ij', centers, books)
        return direct - offset
    codes = lax.map(one_block, (embeds, clusters))
    return (embeds.reshape(ITEMS, D), codes.reshape(ITEMS, CODES))
```

```python
import functools

import jax
import jax.numpy as jnp
from jax import lax
from jax.experimental import pallas as pl
from jax.experimental.pallas import tpu as pltpu
from jax.sharding import PartitionSpec as P

HEADS = 12
EPS = 1e-06
VMEM_BYTES = 56 * 1024 * 1024
F32 = jnp.float32
BF16 = jnp.bfloat16


def params():
    return pltpu.CompilerParams(vmem_limit_bytes=VMEM_BYTES)


def cost(flops, nbytes):
    return pl.CostEstimate(flops=int(flops), bytes_accessed=int(nbytes), transcendentals=0)


def dot(a, b):
    return jnp.dot(a, b, preferred_element_type=F32)


def dot_nt(a, b):
    return lax.dot_general(a, b, (((1,), (1,)), ((), ())), preferred_element_type=F32)


def rms(values, gain):
    mean_sq = jnp.mean(values * values, axis=-1, keepdims=True)
    return values * lax.rsqrt(mean_sq + EPS) * gain


def item_rows(lengths, seq):
    items = lengths.shape[1]
    tri = (
        lax.broadcasted_iota(jnp.int32, (items, items), 0)
        <= lax.broadcasted_iota(jnp.int32, (items, items), 1)
    ).astype(F32)
    rows = jnp.broadcast_to(lengths.astype(F32), (8, items))
    ends = dot(rows.astype(BF16), tri.astype(BF16))[:1]
    starts = ends - rows[:1]
    place = lax.broadcasted_iota(jnp.int32, (seq, items), 0).astype(F32)
    return jnp.where((place < ends) & (place >= starts), 1.0, 0.0).astype(BF16)


def item_columns(lengths, seq):
    items = lengths.shape[1]
    row = lax.broadcasted_iota(jnp.int32, (items, items), 0)
    column = lax.broadcasted_iota(jnp.int32, (items, items), 1)
    rows = jnp.broadcast_to(lengths.astype(F32), (8, items)).astype(BF16)
    ends = dot_nt((column <= row).astype(F32).astype(BF16), rows)[:, :1]
    starts = dot_nt((column < row).astype(F32).astype(BF16), rows)[:, :1]
    place = lax.broadcasted_iota(jnp.int32, (items, seq), 1).astype(F32)
    return jnp.where((place < ends) & (place >= starts), 1.0, 0.0).astype(BF16)


def encoder_kernel(
    lengths_ref, x_ref, wq_ref, wk_ref, wv_ref, wo_ref, gain_ref, gain2_ref,
    normed2_ref, pooled_ref, q_ref, k_ref, v_ref, ctx_ref,
):
    seq, width = x_ref.shape
    lengths = lengths_ref[...]
    head = width // HEADS
    x = x_ref[...].astype(F32)
    normed = rms(x, gain_ref[...]).astype(BF16)
    q_ref[...] = dot(normed, wq_ref[...]).astype(BF16)
    k_ref[...] = dot(normed, wk_ref[...]).astype(BF16)
    v_ref[...] = dot(normed, wv_ref[...]).astype(BF16)
    onehot = item_rows(lengths, seq)
    block, window, lanes = 64, 128, 256
    heads = lanes // head
    lane_head = lax.broadcasted_iota(jnp.int32, (block, lanes), 1) // head
    for start in range(0, seq, block):
        first = min(max(start - (window - block) // 2, 0), seq - window)
        same = dot_nt(onehot[start : start + block], onehot[first : first + window])
        same = jnp.concatenate([same] * heads, axis=0) > 0.5
        for column in range(0, width, lanes):
            query = q_ref[start : start + block, column : column + lanes]
            stacked = jnp.concatenate(
                [jnp.where(lane_head == h, query, jnp.zeros_like(query)) for h in range(heads)], axis=0
            )
            scores = dot_nt(stacked, k_ref[first : first + window, column : column + lanes])
            scores = jnp.where(same, scores, -1e30)
            expo = jnp.exp(scores - jnp.max(scores, axis=-1, keepdims=True))
            probs = (expo / jnp.sum(expo, axis=-1, keepdims=True)).astype(BF16)
            mixed = dot(probs, v_ref[first : first + window, column : column + lanes])
            context = jnp.zeros((block, lanes), F32)
            for h in range(heads):
                context = jnp.where(lane_head == h, mixed[h * block : (h + 1) * block], context)
            ctx_ref[start : start + block, column : column + lanes] = context.astype(BF16)
    stream = (x + dot(ctx_ref[...], wo_ref[...])).astype(BF16)
    normed2_ref[...] = rms(stream.astype(F32), gain2_ref[...]).astype(BF16)
    pooled_ref[...] = dot(item_columns(lengths, seq), stream)


def encode_pack(lengths, x, wq, wk, wv, wo, gain, gain2):
    seq, width = x.shape
    items = lengths.shape[1]
    return pl.pallas_call(
        encoder_kernel,
        out_shape=(
            jax.ShapeDtypeStruct((seq, width), BF16),
            jax.ShapeDtypeStruct((items, width), F32),
        ),
        scratch_shapes=[pltpu.VMEM((seq, width), BF16)] * 4,
        compiler_params=params(),
        cost_estimate=cost(16 * seq * width * width, 8 * width * width + 8 * seq * width),
        name="encode_pack",
    )(lengths, x, wq, wk, wv, wo, gain, gain2)


def feed_kernel(n_in, n_down, has_acc, *refs):
    lengths_refs, normed_refs = refs[0:2], refs[2:4]
    ins, downs = refs[4 : 4 + n_in], refs[4 + n_in : 4 + n_in + n_down]
    rest = refs[4 + n_in + n_down :]
    w_in = jnp.concatenate([r[...] for r in ins], axis=0) if n_in > 1 else ins[0][...]
    w_down = jnp.concatenate([r[...] for r in downs], axis=0) if n_down > 1 else downs[0][...]
    for side in range(2):
        out_ref = rest[-2 + side]
        lengths = lengths_refs[side][...]
        packs, items = lengths.shape
        seq = normed_refs[side].shape[0] // packs
        for pack in range(packs):
            tokens = normed_refs[side][pack * seq : (pack + 1) * seq]
            hidden = jnp.maximum(dot_nt(tokens, w_in), 0.0).astype(BF16)
            pooled = dot(item_columns(lengths[pack : pack + 1], seq), hidden)
            part = dot(pooled.astype(BF16), w_down)
            rows = slice(pack * items, (pack + 1) * items)
            out_ref[rows] = part + rest[side][rows] if has_acc else part


def feed(lengths, normed, w_in, w_down, acc):
    items = lengths[0].shape[0] * lengths[0].shape[1]
    width = normed[0].shape[1]
    units = sum(w.shape[0] for w in w_in)
    tokens = 2 * normed[0].shape[0]
    acc = list(acc) if acc else []
    return pl.pallas_call(
        functools.partial(feed_kernel, len(w_in), len(w_down), bool(acc)),
        out_shape=(jax.ShapeDtypeStruct((items, width), F32),) * 2,
        compiler_params=params(),
        cost_estimate=cost(2 * tokens * width * units * 1.5, 2 * tokens * width + 4 * units * width),
        name="feed",
    )(*lengths, *normed, *w_in, *w_down, *acc)


def place_kernel(acc_ref, other_ref, pooled_ref, gain_ref, slot_ref, cluster_ref, embed_ref, send_ref):
    width = embed_ref.shape[1]
    embed = rms(acc_ref[...] + other_ref[...] + pooled_ref[...], gain_ref[...]).astype(BF16)
    embed_ref[...] = embed
    slots, items = send_ref.shape[0], embed.shape[0]
    placing = jnp.where(
        lax.broadcasted_iota(jnp.int32, (slots, items), 0) == slot_ref[...], 1.0, 0.0
    ).astype(BF16)
    send_ref[:, :width] = dot(placing, embed).astype(BF16)
    clusters = send_ref.shape[1] - width
    chosen = jnp.where(
        lax.broadcasted_iota(jnp.int32, (clusters, items), 0) == cluster_ref[...], 1.0, 0.0
    ).astype(BF16)
    send_ref[:, width:] = dot_nt(placing, chosen).astype(BF16)


def code_kernel(rows_ref, coarse_ref, books_ref, out_ref):
    clusters, codes, width = books_ref.shape
    slots = rows_ref.shape[0]
    rows = rows_ref[:, :width]
    coarse = coarse_ref[...]
    total = jnp.zeros((slots, codes), F32)
    for cluster in range(clusters):
        book = books_ref[cluster]
        offset = dot_nt(coarse, book)[cluster : cluster + 1]
        chosen = rows_ref[:, width + cluster : width + cluster + 1].astype(F32)
        total = total + (dot_nt(rows, book) - offset) * chosen
    out_ref[...] = total.astype(BF16)


def flip(axis_name, count, bits):
    pairs = [(i, i ^ bits) for i in range(count)]
    return lambda value: lax.ppermute(value, axis_name, pairs)


def gather_sixteen(w_input, w_down):
    rows = w_input.shape[0]
    common = rows // 3 // 16 * 16
    half = (rows - common) // 2
    start = common + lax.axis_index("groups") * half

    def mine(weights):
        return lax.dynamic_slice_in_dim(weights, start, half, 0)

    near, far, side = flip("wide", 16, 4), flip("wide", 16, 12), flip("wide", 16, 2)
    twin = flip("groups", 2, 1)
    held = jnp.concatenate([w_input[:common], w_down[:common], mine(w_input), mine(w_down)], axis=0)
    split = 2 * common

    def blocks(main, others):
        w_in = [main[:common], main[split : split + half], others[:half]]
        down = [main[common:split], main[split + half :], others[half:]]
        return w_in, down

    def join(first, second):
        return [a + b for a, b in zip(first, second)]

    side0 = side(held)
    near1 = near(held)
    far2 = far(held)
    x0 = twin(jnp.concatenate([side0[split:], near1[split:]], axis=0))
    side1 = side(near1)
    far3 = near(far2)
    side2 = side(far2)
    x1 = twin(jnp.concatenate([side1[split:], far2[split:]], axis=0))
    side3 = side(far3)
    x2 = twin(jnp.concatenate([side2[split:], far3[split:]], axis=0))
    x3 = twin(side3[split:])
    n = 2 * half
    chunks = [
        join(([w_input], [w_down]), blocks(side0, x0[:n])),
        join(blocks(near1, x0[n:]), blocks(side1, x1[:n])),
        join(blocks(far2, x1[n:]), blocks(side2, x2[:n])),
        join(blocks(far3, x2[n:]), blocks(side3, x3)),
    ]
    return chunks


def gather_any(w_input, w_down, count):
    groups = [list(range(core, count, 2)) for core in range(2)]
    w_in = lax.all_gather(w_input, "wide", axis=0, tiled=True, axis_index_groups=groups)
    down = lax.all_gather(w_down, "wide", axis=0, tiled=True, axis_index_groups=groups)
    return [([w_in], [down])]


def local(
    tokens, item_lengths, w_query, w_key, w_value, w_output, w_input, w_down,
    norm_attn, norm_ffn, norm_final, owner, cluster_slot, coarse, centroids,
):
    packs, seq, width = tokens.shape
    per_pack = item_lengths.shape[1]
    wide_count = lax.axis_size("wide")
    items_dev = packs * per_pack
    capacity = max(2, 2 * items_dev // wide_count)
    slots = wide_count * capacity
    local_clusters, codes_count, _ = centroids.shape
    sibling = flip("wide", wide_count, 1)

    if wide_count == 16:
        chunks = gather_sixteen(w_input, w_down)
    else:
        chunks = gather_any(w_input, w_down, wide_count)

    gain = norm_attn[None]
    gain2 = norm_ffn[None]
    normed, pooled = [], []
    for pack in range(packs):
        a, b = encode_pack(
            item_lengths[pack : pack + 1], tokens[pack], w_query, w_key, w_value, w_output, gain, gain2
        )
        normed.append(a)
        pooled.append(b)
    normed = jnp.concatenate(normed, axis=0)
    pooled = jnp.concatenate(pooled, axis=0)
    both_lengths = (item_lengths, sibling(item_lengths))
    both_normed = (normed, sibling(normed))

    acc = None
    for w_in, down in chunks:
        acc = feed(both_lengths, both_normed, w_in, down, acc)
    other = sibling(acc[1])

    target = owner[:, 0]
    onehot = (target[:, None] == jnp.arange(wide_count, dtype=jnp.int32)[None, :]).astype(jnp.int32)
    earlier = jnp.cumsum(onehot, axis=0) - onehot
    slot_of = target * capacity + jnp.sum(earlier * onehot, axis=1)

    item_embed, send = pl.pallas_call(
        place_kernel,
        out_shape=(
            jax.ShapeDtypeStruct((items_dev, width), BF16),
            jax.ShapeDtypeStruct((slots, width + 128), BF16),
        ),
        compiler_params=params(),
        name="place",
    )(acc[0], other, pooled, norm_final[None], slot_of[None], cluster_slot[None])
    send = send.reshape(wide_count, capacity, width + 128)
    rows = lax.all_to_all(send, "wide", split_axis=0, concat_axis=0, tiled=True)
    codes = pl.pallas_call(
        code_kernel,
        out_shape=jax.ShapeDtypeStruct((slots, codes_count), BF16),
        compiler_params=params(),
        name="codes",
    )(rows.reshape(slots, width + 128), coarse, centroids)
    codes = codes.reshape(wide_count, capacity, codes_count)
    returned = lax.all_to_all(codes, "wide", split_axis=0, concat_axis=0, tiled=True)
    taking = (slot_of[:, None] == jnp.arange(slots, dtype=jnp.int32)[None, :]).astype(BF16)
    item_codes = jnp.dot(taking, returned.reshape(slots, codes_count), preferred_element_type=F32)
    return (item_embed, item_codes)


def solution(mesh):
    return jax.shard_map(
        local,
        mesh=mesh,
        in_specs=(
            P(("groups", "wide"), None, None),
            P(("groups", "wide"), None),
            P(),
            P(),
            P(),
            P(),
            P("wide", None),
            P("wide", None),
            P(),
            P(),
            P(),
            P(("groups", "wide"), None),
            P(("groups", "wide")),
            P("wide", None),
            P("wide", None, None),
        ),
        out_specs=(P(("groups", "wide"), None), P(("groups", "wide"), None)),
        check_vma=False,
    )
```

```python
import functools

import jax
import jax.numpy as jnp
from jax import lax
from jax.experimental import pallas as pl
from jax.experimental.pallas import tpu as pltpu
from jax.sharding import PartitionSpec as P

HEADS = 12
EPS = 1e-06
VMEM_BYTES = 16 * 1024 * 1024
F32 = jnp.float32
BF16 = jnp.bfloat16


def params():
    return pltpu.CompilerParams(vmem_limit_bytes=VMEM_BYTES)


def cost():
    return pl.CostEstimate(flops=1000, bytes_accessed=1000, transcendentals=0)


def dot(a, b):
    return jnp.dot(a, b, preferred_element_type=F32)


def dot_nt(a, b):
    return lax.dot_general(a, b, (((1,), (1,)), ((), ())), preferred_element_type=F32)


def rms(values, gain):
    mean_sq = jnp.mean(values * values, axis=-1, keepdims=True)
    return values * lax.rsqrt(mean_sq + EPS) * gain


def item_rows(lengths, seq):
    items = lengths.shape[1]
    tri = (
        lax.broadcasted_iota(jnp.int32, (items, items), 0)
        <= lax.broadcasted_iota(jnp.int32, (items, items), 1)
    ).astype(F32)
    rows = jnp.broadcast_to(lengths.astype(F32), (8, items))
    ends = dot(rows.astype(BF16), tri.astype(BF16))[:1]
    starts = ends - rows[:1]
    place = lax.broadcasted_iota(jnp.int32, (seq, items), 0).astype(F32)
    return jnp.where((place < ends) & (place >= starts), 1.0, 0.0).astype(BF16)


def item_columns(lengths, seq):
    items = lengths.shape[1]
    row = lax.broadcasted_iota(jnp.int32, (items, items), 0)
    column = lax.broadcasted_iota(jnp.int32, (items, items), 1)
    rows = jnp.broadcast_to(lengths.astype(F32), (8, items)).astype(BF16)
    ends = dot_nt((column <= row).astype(F32).astype(BF16), rows)[:, :1]
    starts = dot_nt((column < row).astype(F32).astype(BF16), rows)[:, :1]
    place = lax.broadcasted_iota(jnp.int32, (items, seq), 1).astype(F32)
    return jnp.where((place < ends) & (place >= starts), 1.0, 0.0).astype(BF16)


def in_hbm(*arrays):
    return [pltpu.with_memory_space_constraint(a, pltpu.HBM) for a in arrays]


def project_kernel(
    other_ref, lengths_hbm, owner_hbm, gain_hbm, x_hbm, wq_hbm, wk_hbm, wv_hbm,
    q_ref, k_ref, v_ref, rows_ref, columns_ref, slot_ref,
    lengths_ref, owner_ref, gain_ref, x_ref, wq_ref, wk_ref, wv_ref, sems, *, wide, capacity,
):
    sources = (lengths_hbm, owner_hbm, gain_hbm, x_hbm, wq_hbm, wk_hbm, wv_hbm)
    here = (lengths_ref, owner_ref, gain_ref, x_ref, wq_ref, wk_ref, wv_ref)
    copies = [pltpu.make_async_copy(s, d, sems.at[i]) for i, (s, d) in enumerate(zip(sources, here))]
    for copy in copies:
        copy.start()
    for copy in copies[:3]:
        copy.wait()
    packs, seq, width = x_ref.shape
    per_pack = lengths_ref.shape[1]
    for pack in range(packs):
        rows_ref[pack * seq : (pack + 1) * seq] = item_rows(lengths_ref[pack : pack + 1], seq)
        for side, ref in enumerate((lengths_ref, other_ref)):
            at = (side * packs + pack) * per_pack
            columns_ref[at : at + per_pack] = item_columns(ref[pack : pack + 1], seq)
    owner = owner_ref[...]
    items = owner.shape[1]
    target = jnp.where(lax.broadcasted_iota(jnp.int32, (wide, items), 0) == owner, 1.0, 0.0)
    before = lax.broadcasted_iota(jnp.int32, (items, items), 0) < lax.broadcasted_iota(jnp.int32, (items, items), 1)
    earlier = dot(target.astype(BF16), jnp.where(before, 1.0, 0.0).astype(BF16))
    rank = jnp.sum(earlier * target, axis=0, keepdims=True)
    slot_ref[...] = owner * capacity + rank.astype(jnp.int32)
    gain = gain_ref[...]
    copies[3].wait()
    normed = [rms(x_ref[pack].astype(F32), gain).astype(BF16) for pack in range(packs)]
    normed = jnp.concatenate(normed, axis=0)
    for copy, w_ref, out_ref in zip(copies[4:], (wq_ref, wk_ref, wv_ref), (q_ref, k_ref, v_ref)):
        copy.wait()
        out_ref[...] = dot(normed, w_ref[...]).astype(BF16)


def project(lengths, other, owner, x, gain, wq, wk, wv, wide, capacity):
    packs, seq, width = x.shape
    items = lengths.shape[1]
    sources = (lengths, owner, gain, x, wq, wk, wv)
    return pl.pallas_call(
        functools.partial(project_kernel, wide=wide, capacity=capacity),
        in_specs=[pl.BlockSpec(memory_space=pltpu.VMEM)] + [pl.BlockSpec(memory_space=pltpu.HBM)] * len(sources),
        out_shape=(
            jax.ShapeDtypeStruct((packs * seq, width), BF16),
            jax.ShapeDtypeStruct((packs * seq, width), BF16),
            jax.ShapeDtypeStruct((packs * seq, width), BF16),
            jax.ShapeDtypeStruct((packs * seq, items), BF16),
            jax.ShapeDtypeStruct((2 * packs * items, seq), BF16),
            jax.ShapeDtypeStruct(owner.shape, jnp.int32),
        ),
        scratch_shapes=[pltpu.VMEM(a.shape, a.dtype) for a in sources]
        + [pltpu.SemaphoreType.DMA((len(sources),))],
        compiler_params=params(),
        cost_estimate=cost(),
        name="project",
    )(other, *in_hbm(*sources))


def hold_kernel(common, group_ref, w_in_hbm, w_down_hbm, held_ref, sems):
    half = (w_in_hbm.shape[0] - common) // 2
    start = pl.multiple_of(common + group_ref[0, 0] * half, 16)
    copies, at = [], 0
    for first, size in ((0, common), (start, half)):
        for source in (w_in_hbm, w_down_hbm):
            copies.append(
                pltpu.make_async_copy(source.at[pl.ds(first, size)], held_ref.at[pl.ds(at, size)], sems.at[len(copies)])
            )
            at += size
    for copy in copies:
        copy.start()
    for copy in copies:
        copy.wait()


def hold(w_input, w_down, common):
    rows, width = w_input.shape
    far = pl.BlockSpec(memory_space=pltpu.HBM)
    return pl.pallas_call(
        functools.partial(hold_kernel, common),
        in_specs=[pl.BlockSpec(memory_space=pltpu.SMEM), far, far],
        out_shape=jax.ShapeDtypeStruct((rows + common, width), BF16),
        scratch_shapes=[pltpu.SemaphoreType.DMA((4,))],
        compiler_params=params(),
        cost_estimate=cost(),
        name="hold",
    )(lax.axis_index("groups").astype(jnp.int32).reshape(1, 1), *in_hbm(w_input, w_down))


def attend_kernel(
    pack, q_ref, k_ref, v_ref, rows_ref, columns_ref, x_ref, wo_ref, gain_ref,
    normed2_ref, pooled_ref, ctx_ref,
):
    _, seq, width = x_ref.shape
    items = rows_ref.shape[1]
    head = width // HEADS
    base = pack * seq
    onehot = rows_ref[base : base + seq]
    block, window, lanes = 64, 128, 256
    heads = lanes // head
    lane_head = lax.broadcasted_iota(jnp.int32, (block, lanes), 1) // head
    for start in range(0, seq, block):
        first = min(max(start - (window - block) // 2, 0), seq - window)
        same = dot_nt(onehot[start : start + block], onehot[first : first + window])
        same = jnp.concatenate([same] * heads, axis=0) > 0.5
        keys = slice(base + first, base + first + window)
        for column in range(0, width, lanes):
            across = slice(column, column + lanes)
            query = q_ref[base + start : base + start + block, across]
            stacked = jnp.concatenate(
                [jnp.where(lane_head == h, query, jnp.zeros_like(query)) for h in range(heads)], axis=0
            )
            scores = jnp.where(same, dot_nt(stacked, k_ref[keys, across]), -1e30)
            expo = jnp.exp(scores - jnp.max(scores, axis=-1, keepdims=True))
            probs = (expo * (1.0 / jnp.sum(expo, axis=-1, keepdims=True))).astype(BF16)
            mixed = dot(probs, v_ref[keys, across])
            context = mixed[:block]
            for h in range(1, heads):
                context = jnp.where(lane_head == h, mixed[h * block : (h + 1) * block], context)
            ctx_ref[start : start + block, across] = context.astype(BF16)
    stream = (x_ref[pack].astype(F32) + dot(ctx_ref[...], wo_ref[...])).astype(BF16)
    normed2_ref[...] = rms(stream.astype(F32), gain_ref[...][None]).astype(BF16)
    pooled_ref[...] = dot(columns_ref[pack * items : (pack + 1) * items], stream)


def attend(pack, projected, x, wo, gain2):
    _, seq, width = x.shape
    items = projected[3].shape[1]
    return pl.pallas_call(
        functools.partial(attend_kernel, pack),
        out_shape=(
            jax.ShapeDtypeStruct((seq, width), BF16),
            jax.ShapeDtypeStruct((items, width), F32),
        ),
        scratch_shapes=[pltpu.VMEM((seq, width), BF16)],
        compiler_params=params(),
        cost_estimate=cost(),
        name="attend",
    )(*projected[:5], x, wo, gain2)


def feed_kernel(n_normed, n_held, pieces, n_base, columns_ref, *refs):
    normed_refs, refs = (refs[:n_normed], refs[n_normed : 2 * n_normed]), refs[2 * n_normed :]
    held, refs = refs[:n_held], refs[n_held:]
    bases, outs = (refs[: n_base[0]], refs[n_base[0] : sum(n_base)]), refs[sum(n_base) :]
    w_in = jnp.concatenate([held[i][r] for i, r, _, _ in pieces], axis=0)
    w_down = jnp.concatenate([held[i][r] for _, _, i, r in pieces], axis=0)
    packs = n_normed
    items = columns_ref.shape[0] // (2 * packs)
    for side in range(2):
        pooled = []
        for pack in range(packs):
            hidden = jnp.maximum(dot_nt(normed_refs[side][pack][...], w_in), 0.0).astype(BF16)
            at = (side * packs + pack) * items
            pooled.append(dot(columns_ref[at : at + items], hidden).astype(BF16))
        part = dot(jnp.concatenate(pooled, axis=0), w_down)
        if bases[side]:
            part = part + jnp.concatenate([r[...] for r in bases[side]], axis=0)
        outs[side][...] = part


def feed(columns, normed, held, pieces, bases):
    items = columns.shape[0] // 2
    width = held[0].shape[1]
    n_base = tuple(len(b) for b in bases)
    return pl.pallas_call(
        functools.partial(feed_kernel, len(normed[0]), len(held), pieces, n_base),
        out_shape=(jax.ShapeDtypeStruct((items, width), F32),) * 2,
        compiler_params=params(),
        cost_estimate=cost(),
        name="feed",
    )(columns, *normed[0], *normed[1], *held, *bases[0], *bases[1])


def place_kernel(acc_ref, other_ref, gain_ref, slot_ref, cluster_ref, embed_ref, send_ref):
    width = embed_ref.shape[1]
    embed = rms(acc_ref[...] + other_ref[...], gain_ref[...][None]).astype(BF16)
    embed_ref[...] = embed
    slots, items = send_ref.shape[0], embed.shape[0]
    placing = jnp.where(
        lax.broadcasted_iota(jnp.int32, (slots, items), 0) == slot_ref[...], 1.0, 0.0
    ).astype(BF16)
    send_ref[:, :width] = dot(placing, embed).astype(BF16)
    clusters = send_ref.shape[1] - width
    chosen = jnp.where(
        lax.broadcasted_iota(jnp.int32, (clusters, items), 0) == cluster_ref[...], 1.0, 0.0
    ).astype(BF16)
    send_ref[:, width:] = dot_nt(placing, chosen).astype(BF16)


def code_kernel(rows_ref, coarse_ref, books_ref, out_ref):
    clusters, codes, width = books_ref.shape
    slots = rows_ref.shape[0]
    spare = -clusters % 16
    coarse = jnp.concatenate([coarse_ref[...], jnp.zeros((spare, width), BF16)], axis=0)
    rows = jnp.concatenate([rows_ref[:, :width], coarse], axis=0)
    total = jnp.zeros((slots, codes), F32)
    for cluster in range(clusters):
        direct = dot_nt(rows, books_ref[cluster])
        offset = direct[slots + cluster : slots + cluster + 1]
        chosen = rows_ref[:, width + cluster : width + cluster + 1].astype(F32)
        total = total + (direct[:slots] - offset) * chosen
    out_ref[...] = total.astype(BF16)


def flip(axis_name, count, bits):
    pairs = [(i, i ^ bits) for i in range(count)]
    return lambda value: lax.ppermute(value, axis_name, pairs)


def gather_any(w_input, w_down, count):
    groups = [list(range(core, count, 2)) for core in range(2)]
    w_in = lax.all_gather(w_input, "wide", axis=0, tiled=True, axis_index_groups=groups)
    down = lax.all_gather(w_down, "wide", axis=0, tiled=True, axis_index_groups=groups)
    return w_in, down


def overlapped(w_input, w_down, tokens, encode_first, encode, sibling):
    rows = w_input.shape[0]
    common = rows // 3 // 16 * 16
    half = (rows - common) // 2
    split, both, every = 2 * common, 2 * half, 2 * (common + half)
    near, side, twin = flip("wide", 16, 4), flip("wide", 16, 2), flip("groups", 2, 1)
    line = lax.axis_index("wide") // 4
    inner = (line == 1) | (line == 2)

    def along(value, hops):
        pairs = [(4 * a + i, 4 * b + i) for a, b in hops for i in range(4)]
        return lax.ppermute(value, "wide", pairs)

    after = lax.optimization_barrier

    def blocks(i):
        return [
            (i, slice(0, common), i, slice(common, split)),
            (i, slice(split, split + half), i, slice(split + half, every)),
        ]

    def rest(i, at=0):
        return [(i, slice(at, at + half), i, slice(at + half, at + both))]

    def cat(a, b):
        return jnp.concatenate([a, b], axis=0)

    held = hold(w_input, w_down, common)
    side0, near1, middle = side(held), near(held), along(held, [(1, 2), (2, 1)])
    projected = encode_first(tokens)
    side0, near1, middle, projected = after((side0, near1, middle, projected))
    columns = projected[4]

    side1 = side(near1)
    far2 = along(jnp.where(inner, middle, held), [(1, 0), (0, 2), (2, 3), (3, 1)])
    x0 = twin(cat(side0[split:], near1[split:]))
    first = encode(0, projected, tokens)
    side1, x0, far2, first, projected = after((side1, x0, far2, first, projected))

    side2, outer = side(far2), along(far2, [(1, 0), (2, 3)])
    x1 = twin(cat(side1[split:], far2[split:]))
    other_first = sibling(first[0])
    second = encode(1, projected, tokens)
    side2, x1, outer, second, other_first = after((side2, x1, outer, second, other_first))

    far3 = jnp.where(inner, middle, outer)
    side3, x2 = side(far3), twin(cat(side2[split:], far3[split:]))
    normed = ((first[0], second[0]), (other_first, sibling(second[0])))
    own = [(0, slice(0, rows), 1, slice(0, rows))]
    pieces = own + blocks(2) + rest(3) + blocks(4) + rest(3, both) + blocks(5) + rest(6)
    acc = feed(columns, normed, [w_input, w_down, side0, x0, near1, side1, x1], pieces, ([first[1], second[1]], []))
    side3, x2, acc = after((side3, x2, acc))

    x3 = twin(side3[split:])
    pieces = blocks(0) + rest(1, both) + blocks(2) + rest(3) + blocks(4) + rest(3, both) + blocks(5)
    acc = feed(columns, normed, [far2, x1, side2, x2, far3, side3], pieces, ([acc[0]], [acc[1]]))
    x3, acc = after((x3, acc))
    acc = feed(columns, normed, [x3], rest(0), ([acc[0]], [acc[1]]))
    return acc, projected[5]


def local(
    tokens, item_lengths, w_query, w_key, w_value, w_output, w_input, w_down,
    norm_attn, norm_ffn, norm_final, owner, cluster_slot, coarse, centroids,
):
    packs, seq, width = tokens.shape
    per_pack = item_lengths.shape[1]
    wide_count = lax.axis_size("wide")
    items_dev = packs * per_pack
    capacity = max(2, 2 * items_dev // wide_count)
    slots = wide_count * capacity
    local_clusters, codes_count, _ = centroids.shape
    sibling = flip("wide", wide_count, 1)

    other_lengths = sibling(item_lengths)

    def encode_first(tokens):
        return project(
            item_lengths, other_lengths, owner.reshape(1, items_dev), tokens, norm_attn[None],
            w_query, w_key, w_value, wide_count, capacity,
        )

    def encode(pack, projected, tokens):
        return attend(pack, projected, tokens, w_output, norm_ffn)

    if wide_count == 16 and packs == 2:
        acc, slots_of = overlapped(w_input, w_down, tokens, encode_first, encode, sibling)
    else:
        projected = encode_first(tokens)
        slots_of = projected[5]
        normed, pooled = zip(*[encode(p, projected, tokens) for p in range(packs)])
        held = gather_any(w_input, w_down, wide_count)
        every = slice(0, held[0].shape[0])
        normed = (normed, [sibling(n) for n in normed])
        acc = feed(projected[4], normed, held, [(0, every, 1, every)], (pooled, []))
    other = sibling(acc[1])

    item_embed, send = pl.pallas_call(
        place_kernel,
        out_shape=(
            jax.ShapeDtypeStruct((items_dev, width), BF16),
            jax.ShapeDtypeStruct((slots, width + 128), BF16),
        ),
        compiler_params=params(),
        name="place",
    )(acc[0], other, norm_final, slots_of, cluster_slot[None])
    send = send.reshape(wide_count, capacity, width + 128)
    rows = lax.all_to_all(send, "wide", split_axis=0, concat_axis=0, tiled=True)
    codes = pl.pallas_call(
        code_kernel,
        out_shape=jax.ShapeDtypeStruct((slots, codes_count), BF16),
        compiler_params=params(),
        name="codes",
    )(rows.reshape(slots, width + 128), coarse, centroids)
    codes = codes.reshape(wide_count, capacity, codes_count)
    returned = lax.all_to_all(codes, "wide", split_axis=0, concat_axis=0, tiled=True)
    taking = (slots_of[0][:, None] == jnp.arange(slots, dtype=jnp.int32)[None, :]).astype(BF16)
    item_codes = jnp.dot(taking, returned.reshape(slots, codes_count), preferred_element_type=F32)
    return (item_embed, item_codes)


def solution(mesh):
    return jax.shard_map(
        local,
        mesh=mesh,
        in_specs=(
            P(("groups", "wide"), None, None),
            P(("groups", "wide"), None),
            P(),
            P(),
            P(),
            P(),
            P("wide", None),
            P("wide", None),
            P(),
            P(),
            P(),
            P(("groups", "wide"), None),
            P(("groups", "wide")),
            P("wide", None),
            P("wide", None, None),
        ),
        out_specs=(P(("groups", "wide"), None), P(("groups", "wide"), None)),
        check_vma=False,
    )
```

```python
import functools

import jax
import jax.numpy as jnp
from jax import lax
from jax.experimental import pallas as pl
from jax.experimental.pallas import tpu as pltpu
from jax.sharding import PartitionSpec as P

HEADS = 12
EPS = 1e-06
VMEM_BYTES = 16 * 1024 * 1024
F32 = jnp.float32
BF16 = jnp.bfloat16


def params():
    return pltpu.CompilerParams(vmem_limit_bytes=VMEM_BYTES)


def cost():
    return pl.CostEstimate(flops=1000, bytes_accessed=1000, transcendentals=0)


def dot(a, b):
    return jnp.dot(a, b, preferred_element_type=F32)


def dot_nt(a, b):
    return lax.dot_general(a, b, (((1,), (1,)), ((), ())), preferred_element_type=F32)


def rms(values, gain):
    mean_sq = jnp.mean(values * values, axis=-1, keepdims=True)
    return values * lax.rsqrt(mean_sq + EPS) * gain


def item_rows(lengths, seq):
    items = lengths.shape[1]
    tri = (
        lax.broadcasted_iota(jnp.int32, (items, items), 0)
        <= lax.broadcasted_iota(jnp.int32, (items, items), 1)
    ).astype(F32)
    rows = jnp.broadcast_to(lengths.astype(F32), (8, items))
    ends = dot(rows.astype(BF16), tri.astype(BF16))[:1]
    starts = ends - rows[:1]
    place = lax.broadcasted_iota(jnp.int32, (seq, items), 0).astype(F32)
    return jnp.where((place < ends) & (place >= starts), 1.0, 0.0).astype(BF16)


def item_columns(lengths, seq):
    items = lengths.shape[1]
    row = lax.broadcasted_iota(jnp.int32, (items, items), 0)
    column = lax.broadcasted_iota(jnp.int32, (items, items), 1)
    rows = jnp.broadcast_to(lengths.astype(F32), (8, items)).astype(BF16)
    ends = dot_nt((column <= row).astype(F32).astype(BF16), rows)[:, :1]
    starts = dot_nt((column < row).astype(F32).astype(BF16), rows)[:, :1]
    place = lax.broadcasted_iota(jnp.int32, (items, seq), 1).astype(F32)
    return jnp.where((place < ends) & (place >= starts), 1.0, 0.0).astype(BF16)


def in_hbm(*arrays):
    return [pltpu.with_memory_space_constraint(a, pltpu.HBM) for a in arrays]


def project_kernel(
    other_ref, lengths_hbm, owner_hbm, gain_hbm, x_hbm, wq_hbm, wk_hbm, wv_hbm,
    q_ref, k_ref, v_ref, rows_ref, columns_ref, slot_ref,
    lengths_ref, owner_ref, gain_ref, x_ref, wq_ref, wk_ref, wv_ref, sems, *, wide, capacity,
):
    sources = (lengths_hbm, owner_hbm, gain_hbm, x_hbm, wq_hbm, wk_hbm, wv_hbm)
    here = (lengths_ref, owner_ref, gain_ref, x_ref, wq_ref, wk_ref, wv_ref)
    copies = [pltpu.make_async_copy(s, d, sems.at[i]) for i, (s, d) in enumerate(zip(sources, here))]
    for copy in copies:
        copy.start()
    for copy in copies[:3]:
        copy.wait()
    packs, seq, width = x_ref.shape
    per_pack = lengths_ref.shape[1]
    for pack in range(packs):
        rows_ref[pack * seq : (pack + 1) * seq] = item_rows(lengths_ref[pack : pack + 1], seq)
        for side, ref in enumerate((lengths_ref, other_ref)):
            at = (side * packs + pack) * per_pack
            columns_ref[at : at + per_pack] = item_columns(ref[pack : pack + 1], seq)
    owner = owner_ref[...]
    items = owner.shape[1]
    target = jnp.where(lax.broadcasted_iota(jnp.int32, (wide, items), 0) == owner, 1.0, 0.0)
    before = lax.broadcasted_iota(jnp.int32, (items, items), 0) < lax.broadcasted_iota(jnp.int32, (items, items), 1)
    earlier = dot(target.astype(BF16), jnp.where(before, 1.0, 0.0).astype(BF16))
    rank = jnp.sum(earlier * target, axis=0, keepdims=True)
    slot_ref[...] = owner * capacity + rank.astype(jnp.int32)
    gain = gain_ref[...][None]
    copies[3].wait()
    normed = [rms(x_ref[pack].astype(F32), gain).astype(BF16) for pack in range(packs)]
    normed = jnp.concatenate(normed, axis=0)
    for copy, w_ref, out_ref in zip(copies[4:], (wq_ref, wk_ref, wv_ref), (q_ref, k_ref, v_ref)):
        copy.wait()
        out_ref[...] = dot(normed, w_ref[...]).astype(BF16)


def project(lengths, other, owner, x, gain, wq, wk, wv, wide, capacity):
    packs, seq, width = x.shape
    items = lengths.shape[1]
    sources = (lengths, owner, gain, x, wq, wk, wv)
    return pl.pallas_call(
        functools.partial(project_kernel, wide=wide, capacity=capacity),
        in_specs=[pl.BlockSpec(memory_space=pltpu.VMEM)] + [pl.BlockSpec(memory_space=pltpu.HBM)] * len(sources),
        out_shape=(
            jax.ShapeDtypeStruct((packs * seq, width), BF16),
            jax.ShapeDtypeStruct((packs * seq, width), BF16),
            jax.ShapeDtypeStruct((packs * seq, width), BF16),
            jax.ShapeDtypeStruct((packs * seq, items), BF16),
            jax.ShapeDtypeStruct((2 * packs * items, seq), BF16),
            jax.ShapeDtypeStruct(owner.shape, jnp.int32),
        ),
        scratch_shapes=[pltpu.VMEM(a.shape, a.dtype) for a in sources]
        + [pltpu.SemaphoreType.DMA((len(sources),))],
        compiler_params=params(),
        cost_estimate=cost(),
        name="project",
    )(other, *in_hbm(*sources))


def hold_kernel(common, group_ref, w_in_hbm, w_down_hbm, held_ref, sems):
    half = (w_in_hbm.shape[0] - common) // 2
    start = pl.multiple_of(common + group_ref[0, 0] * half, 16)
    copies, at = [], 0
    for first, size in ((0, common), (start, half)):
        for source in (w_in_hbm, w_down_hbm):
            copies.append(
                pltpu.make_async_copy(source.at[pl.ds(first, size)], held_ref.at[pl.ds(at, size)], sems.at[len(copies)])
            )
            at += size
    for copy in copies:
        copy.start()
    for copy in copies:
        copy.wait()


def hold(w_input, w_down, common):
    rows, width = w_input.shape
    far = pl.BlockSpec(memory_space=pltpu.HBM)
    return pl.pallas_call(
        functools.partial(hold_kernel, common),
        in_specs=[pl.BlockSpec(memory_space=pltpu.SMEM), far, far],
        out_shape=jax.ShapeDtypeStruct((rows + common, width), BF16),
        scratch_shapes=[pltpu.SemaphoreType.DMA((4,))],
        compiler_params=params(),
        cost_estimate=cost(),
        name="hold",
    )(lax.axis_index("groups").astype(jnp.int32).reshape(1, 1), *in_hbm(w_input, w_down))


def attend_kernel(
    pack, q_ref, k_ref, v_ref, rows_ref, columns_ref, x_ref, wo_ref, gain_ref,
    normed2_ref, pooled_ref, ctx_ref,
):
    _, seq, width = x_ref.shape
    items = rows_ref.shape[1]
    head = width // HEADS
    base = pack * seq
    onehot = rows_ref[base : base + seq]
    block, window, lanes = 64, 128, 256
    heads = lanes // head
    lane_head = lax.broadcasted_iota(jnp.int32, (block, lanes), 1) // head
    for start in range(0, seq, block):
        first = min(max(start - (window - block) // 2, 0), seq - window)
        same = dot_nt(onehot[start : start + block], onehot[first : first + window])
        same = jnp.concatenate([same] * heads, axis=0) > 0.5
        keys = slice(base + first, base + first + window)
        for column in range(0, width, lanes):
            across = slice(column, column + lanes)
            query = q_ref[base + start : base + start + block, across]
            stacked = jnp.concatenate(
                [jnp.where(lane_head == h, query, jnp.zeros_like(query)) for h in range(heads)], axis=0
            )
            scores = jnp.where(same, dot_nt(stacked, k_ref[keys, across]), -1e30)
            expo = jnp.exp(scores - jnp.max(scores, axis=-1, keepdims=True))
            probs = (expo * (1.0 / jnp.sum(expo, axis=-1, keepdims=True))).astype(BF16)
            mixed = dot(probs, v_ref[keys, across])
            context = mixed[:block]
            for h in range(1, heads):
                context = jnp.where(lane_head == h, mixed[h * block : (h + 1) * block], context)
            ctx_ref[start : start + block, across] = context.astype(BF16)
    stream = (x_ref[pack].astype(F32) + dot(ctx_ref[...], wo_ref[...])).astype(BF16)
    normed2_ref[...] = rms(stream.astype(F32), gain_ref[...][None]).astype(BF16)
    pooled_ref[...] = dot(columns_ref[pack * items : (pack + 1) * items], stream)


def attend(pack, projected, x, wo, gain2):
    _, seq, width = x.shape
    items = projected[3].shape[1]
    return pl.pallas_call(
        functools.partial(attend_kernel, pack),
        out_shape=(
            jax.ShapeDtypeStruct((seq, width), BF16),
            jax.ShapeDtypeStruct((items, width), F32),
        ),
        scratch_shapes=[pltpu.VMEM((seq, width), BF16)],
        compiler_params=params(),
        cost_estimate=cost(),
        name="attend",
    )(*projected[:5], x, wo, gain2)


def feed_side_kernel(side, n_held, pieces, columns_ref, *refs):
    normed_refs, held, (base_ref, out_ref) = refs[: -2 - n_held], refs[-2 - n_held : -2], refs[-2:]
    w_in = jnp.concatenate([held[i][r] for i, r, _, _ in pieces], axis=0)
    w_down = jnp.concatenate([held[i][r] for _, _, i, r in pieces], axis=0)
    packs = len(normed_refs)
    items = columns_ref.shape[0] // (2 * packs)
    pooled = []
    for pack in range(packs):
        hidden = jnp.maximum(dot_nt(normed_refs[pack][...], w_in), 0.0).astype(BF16)
        at = (side * packs + pack) * items
        pooled.append(dot(columns_ref[at : at + items], hidden).astype(BF16))
    out_ref[...] = base_ref[...] + dot(jnp.concatenate(pooled, axis=0), w_down)


def feed_side(side, columns, normed, held, pieces, base):
    return pl.pallas_call(
        functools.partial(feed_side_kernel, side, len(held), pieces),
        out_shape=jax.ShapeDtypeStruct(base.shape, F32),
        compiler_params=params(),
        cost_estimate=cost(),
        name="feed_side",
    )(columns, *normed[side], *held, base)


def feed_kernel(n_normed, n_held, pieces, n_base, columns_ref, *refs):
    normed_refs, refs = (refs[:n_normed], refs[n_normed : 2 * n_normed]), refs[2 * n_normed :]
    held, refs = refs[:n_held], refs[n_held:]
    bases, outs = (refs[: n_base[0]], refs[n_base[0] : sum(n_base)]), refs[sum(n_base) :]
    w_in = jnp.concatenate([held[i][r] for i, r, _, _ in pieces], axis=0)
    w_down = jnp.concatenate([held[i][r] for _, _, i, r in pieces], axis=0)
    packs = n_normed
    items = columns_ref.shape[0] // (2 * packs)
    for side in range(2):
        pooled = []
        for pack in range(packs):
            hidden = jnp.maximum(dot_nt(normed_refs[side][pack][...], w_in), 0.0).astype(BF16)
            at = (side * packs + pack) * items
            pooled.append(dot(columns_ref[at : at + items], hidden).astype(BF16))
        part = dot(jnp.concatenate(pooled, axis=0), w_down)
        if bases[side]:
            part = part + jnp.concatenate([r[...] for r in bases[side]], axis=0)
        outs[side][...] = part


def feed(columns, normed, held, pieces, bases):
    items = columns.shape[0] // 2
    width = held[0].shape[1]
    n_base = tuple(len(b) for b in bases)
    return pl.pallas_call(
        functools.partial(feed_kernel, len(normed[0]), len(held), pieces, n_base),
        out_shape=(jax.ShapeDtypeStruct((items, width), F32),) * 2,
        compiler_params=params(),
        cost_estimate=cost(),
        name="feed",
    )(columns, *normed[0], *normed[1], *held, *bases[0], *bases[1])


def place_kernel(acc_ref, other_ref, gain_ref, slot_ref, cluster_ref, embed_ref, send_ref):
    width = embed_ref.shape[1]
    embed = rms(acc_ref[...] + other_ref[...], gain_ref[...][None]).astype(BF16)
    embed_ref[...] = embed
    slots, items = send_ref.shape[0], embed.shape[0]
    placing = jnp.where(
        lax.broadcasted_iota(jnp.int32, (slots, items), 0) == slot_ref[...], 1.0, 0.0
    ).astype(BF16)
    send_ref[:, :width] = dot(placing, embed).astype(BF16)
    clusters = send_ref.shape[1] - width
    chosen = jnp.where(
        lax.broadcasted_iota(jnp.int32, (clusters, items), 0) == cluster_ref[...], 1.0, 0.0
    ).astype(BF16)
    send_ref[:, width:] = dot_nt(placing, chosen).astype(BF16)


def code_kernel(rows_ref, coarse_ref, books_ref, out_ref):
    clusters, codes, width = books_ref.shape
    slots = rows_ref.shape[0]
    spare = -clusters % 16
    coarse = jnp.concatenate([coarse_ref[...], jnp.zeros((spare, width), BF16)], axis=0)
    rows = jnp.concatenate([rows_ref[:, :width], coarse], axis=0)
    total = jnp.zeros((slots, codes), F32)
    for cluster in range(clusters):
        direct = dot_nt(rows, books_ref[cluster])
        offset = direct[slots + cluster : slots + cluster + 1]
        chosen = rows_ref[:, width + cluster : width + cluster + 1].astype(F32)
        total = total + (direct[:slots] - offset) * chosen
    out_ref[...] = total.astype(BF16)


def flip(axis_name, count, bits):
    pairs = [(i, i ^ bits) for i in range(count)]
    return lambda value: lax.ppermute(value, axis_name, pairs)


def gather_any(w_input, w_down, count):
    groups = [list(range(core, count, 2)) for core in range(2)]
    w_in = lax.all_gather(w_input, "wide", axis=0, tiled=True, axis_index_groups=groups)
    down = lax.all_gather(w_down, "wide", axis=0, tiled=True, axis_index_groups=groups)
    return w_in, down


def overlapped(w_input, w_down, tokens, encode_first, encode, sibling):
    rows = w_input.shape[0]
    common = rows // 3 // 16 * 16
    half = (rows - common) // 2
    split, both, every = 2 * common, 2 * half, 2 * (common + half)
    near, side, twin = flip("wide", 16, 4), flip("wide", 16, 2), flip("groups", 2, 1)
    line = lax.axis_index("wide") // 4
    inner = (line == 1) | (line == 2)

    def along(value, hops):
        pairs = [(4 * a + i, 4 * b + i) for a, b in hops for i in range(4)]
        return lax.ppermute(value, "wide", pairs)

    after = lax.optimization_barrier

    def blocks(i):
        return [
            (i, slice(0, common), i, slice(common, split)),
            (i, slice(split, split + half), i, slice(split + half, every)),
        ]

    def rest(i, at=0):
        return [(i, slice(at, at + half), i, slice(at + half, at + both))]

    def cat(a, b):
        return jnp.concatenate([a, b], axis=0)

    held = hold(w_input, w_down, common)
    side0, near1, middle = side(held), near(held), along(held, [(1, 2), (2, 1)])
    projected = encode_first(tokens)
    side0, near1, middle, projected = after((side0, near1, middle, projected))
    columns = projected[4]

    side1 = side(near1)
    far2 = along(jnp.where(inner, middle, held), [(1, 0), (0, 2), (2, 3), (3, 1)])
    x0 = twin(cat(side0[split:], near1[split:]))
    first = encode(0, projected, tokens)
    side1, x0, far2, first, projected = after((side1, x0, far2, first, projected))

    side2, outer = side(far2), along(far2, [(1, 0), (2, 3)])
    x1 = twin(cat(side1[split:], far2[split:]))
    last_inner = along(x0[:both], [(1, 2), (2, 1)])
    other_first = sibling(first[0])
    second = encode(1, projected, tokens)
    side2, x1, outer, last_inner, second, other_first = after((side2, x1, outer, last_inner, second, other_first))

    far3 = jnp.where(inner, middle, outer)
    side3, x2 = side(far3), twin(cat(side2[split:], far3[split:]))
    last_outer = along(x1[:both], [(2, 0), (1, 3)])
    normed = ((first[0], second[0]), (other_first, sibling(second[0])))
    own = [(0, slice(0, rows), 1, slice(0, rows))]
    pieces = own + blocks(2) + rest(3) + blocks(4) + rest(3, both) + blocks(5) + rest(6)
    acc = feed(columns, normed, [w_input, w_down, side0, x0, near1, side1, x1], pieces, ([first[1], second[1]], []))
    pieces = blocks(0) + rest(1, both) + blocks(2) + blocks(3)
    acc = feed(columns, normed, [far2, x1, side2, far3], pieces, ([acc[0]], [acc[1]]))
    side3, x2, last_outer, acc = after((side3, x2, last_outer, acc))

    last = jnp.where(inner, last_inner, last_outer)
    pieces = rest(0) + rest(0, both) + blocks(1) + rest(2)
    held = [x2, side3, last]
    there = sibling(feed_side(1, columns, normed, held, pieces, acc[1]))
    return feed_side(0, columns, normed, held, pieces, acc[0]), there, projected[5]


def local(
    tokens, item_lengths, w_query, w_key, w_value, w_output, w_input, w_down,
    norm_attn, norm_ffn, norm_final, owner, cluster_slot, coarse, centroids,
):
    packs, seq, width = tokens.shape
    per_pack = item_lengths.shape[1]
    wide_count = lax.axis_size("wide")
    items_dev = packs * per_pack
    capacity = max(2, 2 * items_dev // wide_count)
    slots = wide_count * capacity
    local_clusters, codes_count, _ = centroids.shape
    sibling = flip("wide", wide_count, 1)

    other_lengths = sibling(item_lengths)

    def encode_first(tokens):
        return project(
            item_lengths, other_lengths, owner.reshape(1, items_dev), tokens, norm_attn,
            w_query, w_key, w_value, wide_count, capacity,
        )

    def encode(pack, projected, tokens):
        return attend(pack, projected, tokens, w_output, norm_ffn)

    if wide_count == 16 and packs == 2:
        acc, other, slots_of = overlapped(w_input, w_down, tokens, encode_first, encode, sibling)
    else:
        projected = encode_first(tokens)
        slots_of = projected[5]
        normed, pooled = zip(*[encode(p, projected, tokens) for p in range(packs)])
        held = gather_any(w_input, w_down, wide_count)
        every = slice(0, held[0].shape[0])
        normed = (normed, [sibling(n) for n in normed])
        acc = feed(projected[4], normed, held, [(0, every, 1, every)], (pooled, []))
        acc, other = acc[0], sibling(acc[1])

    item_embed, send = pl.pallas_call(
        place_kernel,
        out_shape=(
            jax.ShapeDtypeStruct((items_dev, width), BF16),
            jax.ShapeDtypeStruct((slots, width + 128), BF16),
        ),
        compiler_params=params(),
        name="place",
    )(acc, other, norm_final, slots_of, cluster_slot[None])
    send = send.reshape(wide_count, capacity, width + 128)
    rows = lax.all_to_all(send, "wide", split_axis=0, concat_axis=0, tiled=True)
    codes = pl.pallas_call(
        code_kernel,
        out_shape=jax.ShapeDtypeStruct((slots, codes_count), BF16),
        compiler_params=params(),
        name="codes",
    )(rows.reshape(slots, width + 128), coarse, centroids)
    codes = codes.reshape(wide_count, capacity, codes_count)
    returned = lax.all_to_all(codes, "wide", split_axis=0, concat_axis=0, tiled=True)
    taking = (slots_of[0][:, None] == jnp.arange(slots, dtype=jnp.int32)[None, :]).astype(BF16)
    item_codes = jnp.dot(taking, returned.reshape(slots, codes_count), preferred_element_type=F32)
    return (item_embed, item_codes)


def solution(mesh):
    return jax.shard_map(
        local,
        mesh=mesh,
        in_specs=(
            P(("groups", "wide"), None, None),
            P(("groups", "wide"), None),
            P(),
            P(),
            P(),
            P(),
            P("wide", None),
            P("wide", None),
            P(),
            P(),
            P(),
            P(("groups", "wide"), None),
            P(("groups", "wide")),
            P("wide", None),
            P("wide", None, None),
        ),
        out_specs=(P(("groups", "wide"), None), P(("groups", "wide"), None)),
        check_vma=False,
    )
```

```python
import functools

import jax
import jax.numpy as jnp
from jax import lax
from jax.experimental import pallas as pl
from jax.experimental.pallas import tpu as pltpu
from jax.sharding import PartitionSpec as P

HEADS = 12
EPS = 1e-06
VMEM_BYTES = 16 * 1024 * 1024
F32 = jnp.float32
BF16 = jnp.bfloat16


def params():
    return pltpu.CompilerParams(vmem_limit_bytes=VMEM_BYTES)


def cost():
    return pl.CostEstimate(flops=1000, bytes_accessed=1000, transcendentals=0)


def dot(a, b):
    return jnp.dot(a, b, preferred_element_type=F32)


def dot_nt(a, b):
    return lax.dot_general(a, b, (((1,), (1,)), ((), ())), preferred_element_type=F32)


def rms(values, gain):
    mean_sq = jnp.mean(values * values, axis=-1, keepdims=True)
    return values * lax.rsqrt(mean_sq + EPS) * gain


def item_rows(lengths, seq):
    items = lengths.shape[1]
    tri = (
        lax.broadcasted_iota(jnp.int32, (items, items), 0)
        <= lax.broadcasted_iota(jnp.int32, (items, items), 1)
    ).astype(F32)
    rows = jnp.broadcast_to(lengths.astype(F32), (8, items))
    ends = dot(rows.astype(BF16), tri.astype(BF16))[:1]
    starts = ends - rows[:1]
    place = lax.broadcasted_iota(jnp.int32, (seq, items), 0).astype(F32)
    return jnp.where((place < ends) & (place >= starts), 1.0, 0.0).astype(BF16)


def item_columns(lengths, seq):
    items = lengths.shape[1]
    row = lax.broadcasted_iota(jnp.int32, (items, items), 0)
    column = lax.broadcasted_iota(jnp.int32, (items, items), 1)
    rows = jnp.broadcast_to(lengths.astype(F32), (8, items)).astype(BF16)
    ends = dot_nt((column <= row).astype(F32).astype(BF16), rows)[:, :1]
    starts = dot_nt((column < row).astype(F32).astype(BF16), rows)[:, :1]
    place = lax.broadcasted_iota(jnp.int32, (items, seq), 1).astype(F32)
    return jnp.where((place < ends) & (place >= starts), 1.0, 0.0).astype(BF16)


def in_hbm(*arrays):
    return [pltpu.with_memory_space_constraint(a, pltpu.HBM) for a in arrays]


def project_kernel(
    other_ref, lengths_hbm, owner_hbm, gain_hbm, x_hbm, wq_hbm, wk_hbm, wv_hbm,
    q_ref, k_ref, v_ref, rows_ref, columns_ref, slot_ref,
    lengths_ref, owner_ref, gain_ref, x_ref, wq_ref, wk_ref, wv_ref, sems, *, wide, capacity,
):
    sources = (lengths_hbm, owner_hbm, gain_hbm, x_hbm, wq_hbm, wk_hbm, wv_hbm)
    here = (lengths_ref, owner_ref, gain_ref, x_ref, wq_ref, wk_ref, wv_ref)
    copies = [pltpu.make_async_copy(s, d, sems.at[i]) for i, (s, d) in enumerate(zip(sources, here))]
    for copy in copies:
        copy.start()
    for copy in copies[:3]:
        copy.wait()
    packs, seq, width = x_ref.shape
    per_pack = lengths_ref.shape[1]
    for pack in range(packs):
        rows_ref[pack * seq : (pack + 1) * seq] = item_rows(lengths_ref[pack : pack + 1], seq)
        for side, ref in enumerate((lengths_ref, other_ref)):
            at = (side * packs + pack) * per_pack
            columns_ref[at : at + per_pack] = item_columns(ref[pack : pack + 1], seq)
    owner = owner_ref[...]
    items = owner.shape[1]
    target = jnp.where(lax.broadcasted_iota(jnp.int32, (wide, items), 0) == owner, 1.0, 0.0)
    before = lax.broadcasted_iota(jnp.int32, (items, items), 0) < lax.broadcasted_iota(jnp.int32, (items, items), 1)
    earlier = dot(target.astype(BF16), jnp.where(before, 1.0, 0.0).astype(BF16))
    rank = jnp.sum(earlier * target, axis=0, keepdims=True)
    slot_ref[...] = owner * capacity + rank.astype(jnp.int32)
    gain = gain_ref[...][None]
    copies[3].wait()
    normed = [rms(x_ref[pack].astype(F32), gain).astype(BF16) for pack in range(packs)]
    normed = jnp.concatenate(normed, axis=0)
    for copy, w_ref, out_ref in zip(copies[4:], (wq_ref, wk_ref, wv_ref), (q_ref, k_ref, v_ref)):
        copy.wait()
        out_ref[...] = dot(normed, w_ref[...]).astype(BF16)


def project(lengths, other, owner, x, gain, wq, wk, wv, wide, capacity):
    packs, seq, width = x.shape
    items = lengths.shape[1]
    sources = (lengths, owner, gain, x, wq, wk, wv)
    return pl.pallas_call(
        functools.partial(project_kernel, wide=wide, capacity=capacity),
        in_specs=[pl.BlockSpec(memory_space=pltpu.VMEM)] + [pl.BlockSpec(memory_space=pltpu.HBM)] * len(sources),
        out_shape=(
            jax.ShapeDtypeStruct((packs * seq, width), BF16),
            jax.ShapeDtypeStruct((packs * seq, width), BF16),
            jax.ShapeDtypeStruct((packs * seq, width), BF16),
            jax.ShapeDtypeStruct((packs * seq, items), BF16),
            jax.ShapeDtypeStruct((2 * packs * items, seq), BF16),
            jax.ShapeDtypeStruct(owner.shape, jnp.int32),
        ),
        scratch_shapes=[pltpu.VMEM(a.shape, a.dtype) for a in sources]
        + [pltpu.SemaphoreType.DMA((len(sources),))],
        compiler_params=params(),
        cost_estimate=cost(),
        name="project",
    )(other, *in_hbm(*sources))


def hold_kernel(common, group_ref, w_in_hbm, w_down_hbm, held_ref, sems):
    half = (w_in_hbm.shape[0] - common) // 2
    start = pl.multiple_of(common + group_ref[0, 0] * half, 16)
    copies, at = [], 0
    for first, size in ((0, common), (start, half)):
        for source in (w_in_hbm, w_down_hbm):
            copies.append(
                pltpu.make_async_copy(source.at[pl.ds(first, size)], held_ref.at[pl.ds(at, size)], sems.at[len(copies)])
            )
            at += size
    for copy in copies:
        copy.start()
    for copy in copies:
        copy.wait()


def hold(w_input, w_down, common):
    rows, width = w_input.shape
    far = pl.BlockSpec(memory_space=pltpu.HBM)
    return pl.pallas_call(
        functools.partial(hold_kernel, common),
        in_specs=[pl.BlockSpec(memory_space=pltpu.SMEM), far, far],
        out_shape=jax.ShapeDtypeStruct((rows + common, width), BF16),
        scratch_shapes=[pltpu.SemaphoreType.DMA((4,))],
        compiler_params=params(),
        cost_estimate=cost(),
        name="hold",
    )(lax.axis_index("groups").astype(jnp.int32).reshape(1, 1), *in_hbm(w_input, w_down))


def attend_kernel(
    pack, q_ref, k_ref, v_ref, rows_ref, columns_ref, x_ref, wo_ref, gain_ref,
    normed2_ref, pooled_ref, ctx_ref,
):
    _, seq, width = x_ref.shape
    items = rows_ref.shape[1]
    head = width // HEADS
    base = pack * seq
    onehot = rows_ref[base : base + seq]
    block, window, lanes = 64, 128, 256
    heads = lanes // head
    lane_head = lax.broadcasted_iota(jnp.int32, (block, lanes), 1) // head
    for start in range(0, seq, block):
        first = min(max(start - (window - block) // 2, 0), seq - window)
        same = dot_nt(onehot[start : start + block], onehot[first : first + window])
        same = jnp.concatenate([same] * heads, axis=0) > 0.5
        keys = slice(base + first, base + first + window)
        for column in range(0, width, lanes):
            across = slice(column, column + lanes)
            query = q_ref[base + start : base + start + block, across]
            stacked = jnp.concatenate(
                [jnp.where(lane_head == h, query, jnp.zeros_like(query)) for h in range(heads)], axis=0
            )
            scores = jnp.where(same, dot_nt(stacked, k_ref[keys, across]), -1e30)
            expo = jnp.exp(scores - jnp.max(scores, axis=-1, keepdims=True))
            probs = (expo * (1.0 / jnp.sum(expo, axis=-1, keepdims=True))).astype(BF16)
            mixed = dot(probs, v_ref[keys, across])
            context = mixed[:block]
            for h in range(1, heads):
                context = jnp.where(lane_head == h, mixed[h * block : (h + 1) * block], context)
            ctx_ref[start : start + block, across] = context.astype(BF16)
    stream = (x_ref[pack].astype(F32) + dot(ctx_ref[...], wo_ref[...])).astype(BF16)
    normed2_ref[...] = rms(stream.astype(F32), gain_ref[...][None]).astype(BF16)
    pooled_ref[...] = dot(columns_ref[pack * items : (pack + 1) * items], stream)


def attend(pack, projected, x, wo, gain2):
    _, seq, width = x.shape
    items = projected[3].shape[1]
    return pl.pallas_call(
        functools.partial(attend_kernel, pack),
        out_shape=(
            jax.ShapeDtypeStruct((seq, width), BF16),
            jax.ShapeDtypeStruct((items, width), F32),
        ),
        scratch_shapes=[pltpu.VMEM((seq, width), BF16)],
        compiler_params=params(),
        cost_estimate=cost(),
        name="attend",
    )(*projected[:5], x, wo, gain2)


def feed_side_kernel(side, n_held, pieces, columns_ref, *refs):
    normed_refs, held, (base_ref, out_ref) = refs[: -2 - n_held], refs[-2 - n_held : -2], refs[-2:]
    w_in = jnp.concatenate([held[i][r] for i, r, _, _ in pieces], axis=0)
    w_down = jnp.concatenate([held[i][r] for _, _, i, r in pieces], axis=0)
    packs = len(normed_refs)
    items = columns_ref.shape[0] // (2 * packs)
    pooled = []
    for pack in range(packs):
        hidden = jnp.maximum(dot_nt(normed_refs[pack][...], w_in), 0.0).astype(BF16)
        at = (side * packs + pack) * items
        pooled.append(dot(columns_ref[at : at + items], hidden).astype(BF16))
    out_ref[...] = base_ref[...] + dot(jnp.concatenate(pooled, axis=0), w_down)


def feed_side(side, columns, normed, held, pieces, base):
    return pl.pallas_call(
        functools.partial(feed_side_kernel, side, len(held), pieces),
        out_shape=jax.ShapeDtypeStruct(base.shape, F32),
        compiler_params=params(),
        cost_estimate=cost(),
        name="feed_side",
    )(columns, *normed[side], *held, base)


def feed_kernel(n_normed, n_held, pieces, n_base, columns_ref, *refs):
    normed_refs, refs = (refs[:n_normed], refs[n_normed : 2 * n_normed]), refs[2 * n_normed :]
    held, refs = refs[:n_held], refs[n_held:]
    bases, outs = (refs[: n_base[0]], refs[n_base[0] : sum(n_base)]), refs[sum(n_base) :]
    w_in = jnp.concatenate([held[i][r] for i, r, _, _ in pieces], axis=0)
    w_down = jnp.concatenate([held[i][r] for _, _, i, r in pieces], axis=0)
    packs = n_normed
    items = columns_ref.shape[0] // (2 * packs)
    for side in range(2):
        pooled = []
        for pack in range(packs):
            hidden = jnp.maximum(dot_nt(normed_refs[side][pack][...], w_in), 0.0).astype(BF16)
            at = (side * packs + pack) * items
            pooled.append(dot(columns_ref[at : at + items], hidden).astype(BF16))
        part = dot(jnp.concatenate(pooled, axis=0), w_down)
        if bases[side]:
            part = part + jnp.concatenate([r[...] for r in bases[side]], axis=0)
        outs[side][...] = part


def feed(columns, normed, held, pieces, bases):
    items = columns.shape[0] // 2
    width = held[0].shape[1]
    n_base = tuple(len(b) for b in bases)
    return pl.pallas_call(
        functools.partial(feed_kernel, len(normed[0]), len(held), pieces, n_base),
        out_shape=(jax.ShapeDtypeStruct((items, width), F32),) * 2,
        compiler_params=params(),
        cost_estimate=cost(),
        name="feed",
    )(columns, *normed[0], *normed[1], *held, *bases[0], *bases[1])


def place_kernel(acc_ref, other_ref, gain_ref, slot_ref, cluster_ref, embed_ref, send_ref):
    width = embed_ref.shape[1]
    embed = rms(acc_ref[...] + other_ref[...], gain_ref[...][None]).astype(BF16)
    embed_ref[...] = embed
    slots, items = send_ref.shape[0], embed.shape[0]
    placing = jnp.where(
        lax.broadcasted_iota(jnp.int32, (slots, items), 0) == slot_ref[...], 1.0, 0.0
    ).astype(BF16)
    send_ref[:, :width] = dot(placing, embed).astype(BF16)
    clusters = send_ref.shape[1] - width
    chosen = jnp.where(
        lax.broadcasted_iota(jnp.int32, (clusters, items), 0) == cluster_ref[...], 1.0, 0.0
    ).astype(BF16)
    send_ref[:, width:] = dot_nt(placing, chosen).astype(BF16)


def code_kernel(rows_ref, coarse_ref, books_ref, out_ref):
    clusters, codes, width = books_ref.shape
    slots = rows_ref.shape[0]
    spare = -clusters % 16
    coarse = jnp.concatenate([coarse_ref[...], jnp.zeros((spare, width), BF16)], axis=0)
    rows = jnp.concatenate([rows_ref[:, :width], coarse], axis=0)
    total = jnp.zeros((slots, codes), F32)
    for cluster in range(clusters):
        direct = dot_nt(rows, books_ref[cluster])
        offset = direct[slots + cluster : slots + cluster + 1]
        chosen = rows_ref[:, width + cluster : width + cluster + 1].astype(F32)
        total = total + (direct[:slots] - offset) * chosen
    out_ref[...] = total.astype(BF16)


def flip(axis_name, count, bits):
    pairs = [(i, i ^ bits) for i in range(count)]
    return lambda value: lax.ppermute(value, axis_name, pairs)


def gather_any(w_input, w_down, count):
    groups = [list(range(core, count, 2)) for core in range(2)]
    w_in = lax.all_gather(w_input, "wide", axis=0, tiled=True, axis_index_groups=groups)
    down = lax.all_gather(w_down, "wide", axis=0, tiled=True, axis_index_groups=groups)
    return w_in, down


def overlapped(w_input, w_down, tokens, encode_first, encode, sibling):
    rows = w_input.shape[0]
    common = rows // 3 // 16 * 16
    half = (rows - common) // 2
    split, both, every = 2 * common, 2 * half, 2 * (common + half)
    near, side, twin = flip("wide", 16, 4), flip("wide", 16, 2), flip("groups", 2, 1)
    line = lax.axis_index("wide") // 4
    inner = (line == 1) | (line == 2)

    def along(value, hops):
        pairs = [(4 * a + i, 4 * b + i) for a, b in hops for i in range(4)]
        return lax.ppermute(value, "wide", pairs)

    def amid(value):
        pairs = [(i, i ^ 12 if i // 4 in (1, 2) else i ^ 1) for i in range(16)]
        return lax.ppermute(value, "wide", pairs)

    after = lax.optimization_barrier

    def blocks(i):
        return [
            (i, slice(0, common), i, slice(common, split)),
            (i, slice(split, split + half), i, slice(split + half, every)),
        ]

    def rest(i, at=0):
        return [(i, slice(at, at + half), i, slice(at + half, at + both))]

    def cat(a, b):
        return jnp.concatenate([a, b], axis=0)

    held = hold(w_input, w_down, common)
    side0, near1, middle = side(held), near(held), amid(held)
    projected = encode_first(tokens)
    side0, near1, middle, projected = after((side0, near1, middle, projected))
    columns = projected[4]

    side1 = side(near1)
    far2 = along(jnp.where(inner, middle, held), [(1, 0), (0, 2), (2, 3), (3, 1)])
    x0 = twin(cat(side0[split:], near1[split:]))
    first = encode(0, projected, tokens)
    side1, x0, far2, first, projected = after((side1, x0, far2, first, projected))

    side2, outer = side(far2), near(far2)
    x1 = twin(cat(side1[split:], far2[split:]))
    last_inner = amid(x0[:both])
    other_first = sibling(first[0])
    second = encode(1, projected, tokens)
    side2, x1, outer, last_inner, second, other_first = after((side2, x1, outer, last_inner, second, other_first))

    far3 = jnp.where(inner, middle, outer)
    side3, x2 = side(far3), twin(cat(side2[split:], far3[split:]))
    last_outer = along(x1[:both], [(2, 0), (1, 3)])
    normed = ((first[0], second[0]), (other_first, sibling(second[0])))
    own = [(0, slice(0, rows), 1, slice(0, rows))]
    pieces = own + blocks(2) + rest(3) + blocks(4) + rest(3, both) + blocks(5) + rest(6)
    acc = feed(columns, normed, [w_input, w_down, side0, x0, near1, side1, x1], pieces, ([first[1], second[1]], []))
    pieces = blocks(0) + rest(1, both) + blocks(2) + blocks(3)
    acc = feed(columns, normed, [far2, x1, side2, far3], pieces, ([acc[0]], [acc[1]]))
    side3, x2, last_outer, acc = after((side3, x2, last_outer, acc))

    last = jnp.where(inner, last_inner, last_outer)
    pieces = rest(0) + rest(0, both) + blocks(1) + rest(2)
    held = [x2, side3, last]
    there = sibling(feed_side(1, columns, normed, held, pieces, acc[1]))
    return feed_side(0, columns, normed, held, pieces, acc[0]), there, projected[5]


def local(
    tokens, item_lengths, w_query, w_key, w_value, w_output, w_input, w_down,
    norm_attn, norm_ffn, norm_final, owner, cluster_slot, coarse, centroids,
):
    packs, seq, width = tokens.shape
    per_pack = item_lengths.shape[1]
    wide_count = lax.axis_size("wide")
    items_dev = packs * per_pack
    capacity = max(2, 2 * items_dev // wide_count)
    slots = wide_count * capacity
    local_clusters, codes_count, _ = centroids.shape
    sibling = flip("wide", wide_count, 1)

    other_lengths = sibling(item_lengths)

    def encode_first(tokens):
        return project(
            item_lengths, other_lengths, owner.reshape(1, items_dev), tokens, norm_attn,
            w_query, w_key, w_value, wide_count, capacity,
        )

    def encode(pack, projected, tokens):
        return attend(pack, projected, tokens, w_output, norm_ffn)

    if wide_count == 16 and packs == 2:
        acc, other, slots_of = overlapped(w_input, w_down, tokens, encode_first, encode, sibling)
    else:
        projected = encode_first(tokens)
        slots_of = projected[5]
        normed, pooled = zip(*[encode(p, projected, tokens) for p in range(packs)])
        held = gather_any(w_input, w_down, wide_count)
        every = slice(0, held[0].shape[0])
        normed = (normed, [sibling(n) for n in normed])
        acc = feed(projected[4], normed, held, [(0, every, 1, every)], (pooled, []))
        acc, other = acc[0], sibling(acc[1])

    item_embed, send = pl.pallas_call(
        place_kernel,
        out_shape=(
            jax.ShapeDtypeStruct((items_dev, width), BF16),
            jax.ShapeDtypeStruct((slots, width + 128), BF16),
        ),
        compiler_params=params(),
        name="place",
    )(acc, other, norm_final, slots_of, cluster_slot[None])
    send = send.reshape(wide_count, capacity, width + 128)
    rows = lax.all_to_all(send, "wide", split_axis=0, concat_axis=0, tiled=True)
    codes = pl.pallas_call(
        code_kernel,
        out_shape=jax.ShapeDtypeStruct((slots, codes_count), BF16),
        compiler_params=params(),
        name="codes",
    )(rows.reshape(slots, width + 128), coarse, centroids)
    codes = codes.reshape(wide_count, capacity, codes_count)
    returned = lax.all_to_all(codes, "wide", split_axis=0, concat_axis=0, tiled=True)
    taking = (slots_of[0][:, None] == jnp.arange(slots, dtype=jnp.int32)[None, :]).astype(BF16)
    item_codes = jnp.dot(taking, returned.reshape(slots, codes_count), preferred_element_type=F32)
    return (item_embed, item_codes)


def solution(mesh):
    return jax.shard_map(
        local,
        mesh=mesh,
        in_specs=(
            P(("groups", "wide"), None, None),
            P(("groups", "wide"), None),
            P(),
            P(),
            P(),
            P(),
            P("wide", None),
            P("wide", None),
            P(),
            P(),
            P(),
            P(("groups", "wide"), None),
            P(("groups", "wide")),
            P("wide", None),
            P("wide", None, None),
        ),
        out_specs=(P(("groups", "wide"), None), P(("groups", "wide"), None)),
        check_vma=False,
    )
```

```python
import functools

import jax
import jax.numpy as jnp
from jax import lax
from jax.experimental import pallas as pl
from jax.experimental.pallas import tpu as pltpu
from jax.sharding import PartitionSpec as P

HEADS = 12
EPS = 1e-06
VMEM_BYTES = 16 * 1024 * 1024
F32 = jnp.float32
BF16 = jnp.bfloat16


def params():
    return pltpu.CompilerParams(vmem_limit_bytes=VMEM_BYTES)


def cost():
    return pl.CostEstimate(flops=1000, bytes_accessed=1000, transcendentals=0)


def dot(a, b):
    return jnp.dot(a, b, preferred_element_type=F32)


def dot_nt(a, b):
    return lax.dot_general(a, b, (((1,), (1,)), ((), ())), preferred_element_type=F32)


def rms(values, gain):
    mean_sq = jnp.mean(values * values, axis=-1, keepdims=True)
    return values * lax.rsqrt(mean_sq + EPS) * gain


def item_rows(lengths, seq):
    items = lengths.shape[1]
    tri = (
        lax.broadcasted_iota(jnp.int32, (items, items), 0)
        <= lax.broadcasted_iota(jnp.int32, (items, items), 1)
    ).astype(F32)
    rows = jnp.broadcast_to(lengths.astype(F32), (8, items))
    ends = dot(rows.astype(BF16), tri.astype(BF16))[:1]
    starts = ends - rows[:1]
    place = lax.broadcasted_iota(jnp.int32, (seq, items), 0).astype(F32)
    return jnp.where((place < ends) & (place >= starts), 1.0, 0.0).astype(BF16)


def item_columns(lengths, seq):
    items = lengths.shape[1]
    row = lax.broadcasted_iota(jnp.int32, (items, items), 0)
    column = lax.broadcasted_iota(jnp.int32, (items, items), 1)
    rows = jnp.broadcast_to(lengths.astype(F32), (8, items)).astype(BF16)
    ends = dot_nt((column <= row).astype(F32).astype(BF16), rows)[:, :1]
    starts = dot_nt((column < row).astype(F32).astype(BF16), rows)[:, :1]
    place = lax.broadcasted_iota(jnp.int32, (items, seq), 1).astype(F32)
    return jnp.where((place < ends) & (place >= starts), 1.0, 0.0).astype(BF16)


def in_hbm(*arrays):
    return [pltpu.with_memory_space_constraint(a, pltpu.HBM) for a in arrays]


def project_kernel(
    other_ref, lengths_hbm, owner_hbm, gain_hbm, x_hbm, wq_hbm, wk_hbm, wv_hbm,
    q_ref, k_ref, v_ref, rows_ref, columns_ref, slot_ref,
    lengths_ref, owner_ref, gain_ref, x_ref, wq_ref, wk_ref, wv_ref, sems, *, wide, capacity,
):
    sources = (lengths_hbm, owner_hbm, gain_hbm, x_hbm, wq_hbm, wk_hbm, wv_hbm)
    here = (lengths_ref, owner_ref, gain_ref, x_ref, wq_ref, wk_ref, wv_ref)
    copies = [pltpu.make_async_copy(s, d, sems.at[i]) for i, (s, d) in enumerate(zip(sources, here))]
    for copy in copies:
        copy.start()
    for copy in copies[:3]:
        copy.wait()
    packs, seq, width = x_ref.shape
    per_pack = lengths_ref.shape[1]
    for pack in range(packs):
        rows_ref[pack * seq : (pack + 1) * seq] = item_rows(lengths_ref[pack : pack + 1], seq)
        for side, ref in enumerate((lengths_ref, other_ref)):
            at = (side * packs + pack) * per_pack
            columns_ref[at : at + per_pack] = item_columns(ref[pack : pack + 1], seq)
    owner = owner_ref[...]
    items = owner.shape[1]
    target = jnp.where(lax.broadcasted_iota(jnp.int32, (wide, items), 0) == owner, 1.0, 0.0)
    before = lax.broadcasted_iota(jnp.int32, (items, items), 0) < lax.broadcasted_iota(jnp.int32, (items, items), 1)
    earlier = dot(target.astype(BF16), jnp.where(before, 1.0, 0.0).astype(BF16))
    rank = jnp.sum(earlier * target, axis=0, keepdims=True)
    slot_ref[...] = owner * capacity + rank.astype(jnp.int32)
    gain = gain_ref[...][None]
    copies[3].wait()
    normed = [rms(x_ref[pack].astype(F32), gain).astype(BF16) for pack in range(packs)]
    normed = jnp.concatenate(normed, axis=0)
    for copy, w_ref, out_ref in zip(copies[4:], (wq_ref, wk_ref, wv_ref), (q_ref, k_ref, v_ref)):
        copy.wait()
        out_ref[...] = dot(normed, w_ref[...]).astype(BF16)


def project(lengths, other, owner, x, gain, wq, wk, wv, wide, capacity):
    packs, seq, width = x.shape
    items = lengths.shape[1]
    sources = (lengths, owner, gain, x, wq, wk, wv)
    return pl.pallas_call(
        functools.partial(project_kernel, wide=wide, capacity=capacity),
        in_specs=[pl.BlockSpec(memory_space=pltpu.VMEM)] + [pl.BlockSpec(memory_space=pltpu.HBM)] * len(sources),
        out_shape=(
            jax.ShapeDtypeStruct((packs * seq, width), BF16),
            jax.ShapeDtypeStruct((packs * seq, width), BF16),
            jax.ShapeDtypeStruct((packs * seq, width), BF16),
            jax.ShapeDtypeStruct((packs * seq, items), BF16),
            jax.ShapeDtypeStruct((2 * packs * items, seq), BF16),
            jax.ShapeDtypeStruct(owner.shape, jnp.int32),
        ),
        scratch_shapes=[pltpu.VMEM(a.shape, a.dtype) for a in sources]
        + [pltpu.SemaphoreType.DMA((len(sources),))],
        compiler_params=params(),
        cost_estimate=cost(),
        name="project",
    )(other, *in_hbm(*sources))


def hold_kernel(common, group_ref, w_in_hbm, w_down_hbm, held_ref, sems):
    half = (w_in_hbm.shape[0] - common) // 2
    start = pl.multiple_of(common + group_ref[0, 0] * half, 16)
    copies, at = [], 0
    for first, size in ((0, common), (start, half)):
        for source in (w_in_hbm, w_down_hbm):
            copies.append(
                pltpu.make_async_copy(source.at[pl.ds(first, size)], held_ref.at[pl.ds(at, size)], sems.at[len(copies)])
            )
            at += size
    for copy in copies:
        copy.start()
    for copy in copies:
        copy.wait()


def hold(w_input, w_down, common):
    rows, width = w_input.shape
    far = pl.BlockSpec(memory_space=pltpu.HBM)
    return pl.pallas_call(
        functools.partial(hold_kernel, common),
        in_specs=[pl.BlockSpec(memory_space=pltpu.SMEM), far, far],
        out_shape=jax.ShapeDtypeStruct((rows + common, width), BF16),
        scratch_shapes=[pltpu.SemaphoreType.DMA((4,))],
        compiler_params=params(),
        cost_estimate=cost(),
        name="hold",
    )(lax.axis_index("groups").astype(jnp.int32).reshape(1, 1), *in_hbm(w_input, w_down))


def attend_kernel(
    pack, q_ref, k_ref, v_ref, rows_ref, columns_ref, x_ref, wo_ref, gain_ref,
    normed2_ref, pooled_ref, ctx_ref,
):
    _, seq, width = x_ref.shape
    items = rows_ref.shape[1]
    head = width // HEADS
    base = pack * seq
    onehot = rows_ref[base : base + seq]
    block, window, lanes = 64, 128, 256
    heads = lanes // head
    lane_head = lax.broadcasted_iota(jnp.int32, (block, lanes), 1) // head
    for start in range(0, seq, block):
        first = min(max(start - (window - block) // 2, 0), seq - window)
        same = dot_nt(onehot[start : start + block], onehot[first : first + window])
        same = jnp.concatenate([same] * heads, axis=0) > 0.5
        keys = slice(base + first, base + first + window)
        for column in range(0, width, lanes):
            across = slice(column, column + lanes)
            query = q_ref[base + start : base + start + block, across]
            stacked = jnp.concatenate(
                [jnp.where(lane_head == h, query, jnp.zeros_like(query)) for h in range(heads)], axis=0
            )
            scores = jnp.where(same, dot_nt(stacked, k_ref[keys, across]), -1e30)
            expo = jnp.exp(scores - jnp.max(scores, axis=-1, keepdims=True))
            probs = (expo * (1.0 / jnp.sum(expo, axis=-1, keepdims=True))).astype(BF16)
            mixed = dot(probs, v_ref[keys, across])
            context = mixed[:block]
            for h in range(1, heads):
                context = jnp.where(lane_head == h, mixed[h * block : (h + 1) * block], context)
            ctx_ref[start : start + block, across] = context.astype(BF16)
    stream = (x_ref[pack].astype(F32) + dot(ctx_ref[...], wo_ref[...])).astype(BF16)
    normed2_ref[...] = rms(stream.astype(F32), gain_ref[...][None]).astype(BF16)
    pooled_ref[...] = dot(columns_ref[pack * items : (pack + 1) * items], stream)


def attend(pack, projected, x, wo, gain2):
    _, seq, width = x.shape
    items = projected[3].shape[1]
    return pl.pallas_call(
        functools.partial(attend_kernel, pack),
        out_shape=(
            jax.ShapeDtypeStruct((seq, width), BF16),
            jax.ShapeDtypeStruct((items, width), F32),
        ),
        scratch_shapes=[pltpu.VMEM((seq, width), BF16)],
        compiler_params=params(),
        cost_estimate=cost(),
        name="attend",
    )(*projected[:5], x, wo, gain2)


def feed_side_kernel(side, n_held, pieces, columns_ref, *refs):
    normed_refs, held, (base_ref, out_ref) = refs[: -2 - n_held], refs[-2 - n_held : -2], refs[-2:]
    w_in = jnp.concatenate([held[i][r] for i, r, _, _ in pieces], axis=0)
    w_down = jnp.concatenate([held[i][r] for _, _, i, r in pieces], axis=0)
    packs = len(normed_refs)
    items = columns_ref.shape[0] // (2 * packs)
    pooled = []
    for pack in range(packs):
        hidden = jnp.maximum(dot_nt(normed_refs[pack][...], w_in), 0.0).astype(BF16)
        at = (side * packs + pack) * items
        pooled.append(dot(columns_ref[at : at + items], hidden).astype(BF16))
    out_ref[...] = base_ref[...] + dot(jnp.concatenate(pooled, axis=0), w_down)


def feed_side(side, columns, normed, held, pieces, base):
    return pl.pallas_call(
        functools.partial(feed_side_kernel, side, len(held), pieces),
        out_shape=jax.ShapeDtypeStruct(base.shape, F32),
        compiler_params=params(),
        cost_estimate=cost(),
        name="feed_side",
    )(columns, *normed[side], *held, base)


def feed_kernel(n_normed, n_held, pieces, n_base, columns_ref, *refs):
    normed_refs, refs = (refs[:n_normed], refs[n_normed : 2 * n_normed]), refs[2 * n_normed :]
    held, refs = refs[:n_held], refs[n_held:]
    bases, outs = (refs[: n_base[0]], refs[n_base[0] : sum(n_base)]), refs[sum(n_base) :]
    w_in = jnp.concatenate([held[i][r] for i, r, _, _ in pieces], axis=0)
    w_down = jnp.concatenate([held[i][r] for _, _, i, r in pieces], axis=0)
    packs = n_normed
    items = columns_ref.shape[0] // (2 * packs)
    for side in range(2):
        pooled = []
        for pack in range(packs):
            hidden = jnp.maximum(dot_nt(normed_refs[side][pack][...], w_in), 0.0).astype(BF16)
            at = (side * packs + pack) * items
            pooled.append(dot(columns_ref[at : at + items], hidden).astype(BF16))
        part = dot(jnp.concatenate(pooled, axis=0), w_down)
        if bases[side]:
            part = part + jnp.concatenate([r[...] for r in bases[side]], axis=0)
        outs[side][...] = part


def feed(columns, normed, held, pieces, bases):
    items = columns.shape[0] // 2
    width = held[0].shape[1]
    n_base = tuple(len(b) for b in bases)
    return pl.pallas_call(
        functools.partial(feed_kernel, len(normed[0]), len(held), pieces, n_base),
        out_shape=(jax.ShapeDtypeStruct((items, width), F32),) * 2,
        compiler_params=params(),
        cost_estimate=cost(),
        name="feed",
    )(columns, *normed[0], *normed[1], *held, *bases[0], *bases[1])


def place_kernel(acc_ref, other_ref, gain_ref, slot_ref, cluster_ref, embed_ref, send_ref):
    width = embed_ref.shape[1]
    embed = rms(acc_ref[...] + other_ref[...], gain_ref[...][None]).astype(BF16)
    embed_ref[...] = embed
    slots, items = send_ref.shape[0], embed.shape[0]
    placing = jnp.where(
        lax.broadcasted_iota(jnp.int32, (slots, items), 0) == slot_ref[...], 1.0, 0.0
    ).astype(BF16)
    send_ref[:, :width] = dot(placing, embed).astype(BF16)
    clusters = send_ref.shape[1] - width
    chosen = jnp.where(
        lax.broadcasted_iota(jnp.int32, (clusters, items), 0) == cluster_ref[...], 1.0, 0.0
    ).astype(BF16)
    send_ref[:, width:] = dot_nt(placing, chosen).astype(BF16)


def code_kernel(rows_ref, coarse_ref, books_ref, out_ref):
    clusters, codes, width = books_ref.shape
    slots = rows_ref.shape[0]
    spare = -clusters % 16
    coarse = jnp.concatenate([coarse_ref[...], jnp.zeros((spare, width), BF16)], axis=0)
    rows = jnp.concatenate([rows_ref[:, :width], coarse], axis=0)
    total = jnp.zeros((slots, codes), F32)
    for cluster in range(clusters):
        direct = dot_nt(rows, books_ref[cluster])
        offset = direct[slots + cluster : slots + cluster + 1]
        chosen = rows_ref[:, width + cluster : width + cluster + 1].astype(F32)
        total = total + (direct[:slots] - offset) * chosen
    out_ref[...] = total.astype(BF16)


def flip(axis_name, count, bits):
    pairs = [(i, i ^ bits) for i in range(count)]
    return lambda value: lax.ppermute(value, axis_name, pairs)


def gather_any(w_input, w_down, count):
    groups = [list(range(core, count, 2)) for core in range(2)]
    w_in = lax.all_gather(w_input, "wide", axis=0, tiled=True, axis_index_groups=groups)
    down = lax.all_gather(w_down, "wide", axis=0, tiled=True, axis_index_groups=groups)
    return w_in, down


def overlapped(w_input, w_down, tokens, encode_first, encode, sibling):
    rows = w_input.shape[0]
    common = rows // 3 // 16 * 16
    half = (rows - common) // 2
    split, both, every = 2 * common, 2 * half, 2 * (common + half)
    near, side, twin = flip("wide", 16, 4), flip("wide", 16, 2), flip("groups", 2, 1)
    line = lax.axis_index("wide") // 4
    inner = (line == 1) | (line == 2)

    def along(value, hops):
        pairs = [(4 * a + i, 4 * b + i) for a, b in hops for i in range(4)]
        return lax.ppermute(value, "wide", pairs)

    def amid(value):
        pairs = [(i, i ^ 12 if i // 4 in (1, 2) else i ^ 1) for i in range(16)]
        return lax.ppermute(value, "wide", pairs)

    after = lax.optimization_barrier

    def blocks(i):
        return [
            (i, slice(0, common), i, slice(common, split)),
            (i, slice(split, split + half), i, slice(split + half, every)),
        ]

    def rest(i, at=0):
        return [(i, slice(at, at + half), i, slice(at + half, at + both))]

    def cat(a, b):
        return jnp.concatenate([a, b], axis=0)

    held = hold(w_input, w_down, common)
    side0, near1, middle = side(held), near(held), amid(held)
    projected = encode_first(tokens)
    side0, near1, middle, projected = after((side0, near1, middle, projected))
    columns = projected[4]

    side1 = side(near1)
    far2 = along(jnp.where(inner, middle, held), [(1, 0), (0, 2), (2, 3), (3, 1)])
    x0 = twin(cat(side0[split:], near1[split:]))
    first = encode(0, projected, tokens)
    side1, x0, far2, first, projected = after((side1, x0, far2, first, projected))

    side2, outer = side(far2), near(far2)
    x1 = twin(cat(side1[split:], far2[split:]))
    last_inner = amid(x0[:both])
    second = encode(1, projected, tokens)
    side2, x1, outer, last_inner, second = after((side2, x1, outer, last_inner, second))

    far3 = jnp.where(inner, middle, outer)
    side3, x2 = side(far3), twin(cat(side2[split:], far3[split:]))
    last_outer = along(x1[:both], [(2, 0), (1, 3)])
    normed = ((first[0], second[0]), (sibling(first[0]), sibling(second[0])))
    own = [(0, slice(0, rows), 1, slice(0, rows))]
    pieces = own + blocks(2) + rest(3) + blocks(4) + rest(3, both) + blocks(5) + rest(6)
    acc = feed(columns, normed, [w_input, w_down, side0, x0, near1, side1, x1], pieces, ([first[1], second[1]], []))
    pieces = blocks(0) + rest(1, both) + blocks(2) + blocks(3)
    acc = feed(columns, normed, [far2, x1, side2, far3], pieces, ([acc[0]], [acc[1]]))
    side3, x2, last_outer, acc = after((side3, x2, last_outer, acc))

    last = jnp.where(inner, last_inner, last_outer)
    pieces = rest(0) + rest(0, both) + blocks(1) + rest(2)
    held = [x2, side3, last]
    there = sibling(feed_side(1, columns, normed, held, pieces, acc[1]))
    return feed_side(0, columns, normed, held, pieces, acc[0]), there, projected[5]


def local(
    tokens, item_lengths, w_query, w_key, w_value, w_output, w_input, w_down,
    norm_attn, norm_ffn, norm_final, owner, cluster_slot, coarse, centroids,
):
    packs, seq, width = tokens.shape
    per_pack = item_lengths.shape[1]
    wide_count = lax.axis_size("wide")
    items_dev = packs * per_pack
    capacity = max(2, 2 * items_dev // wide_count)
    slots = wide_count * capacity
    local_clusters, codes_count, _ = centroids.shape
    sibling = flip("wide", wide_count, 1)

    other_lengths = sibling(item_lengths)

    def encode_first(tokens):
        return project(
            item_lengths, other_lengths, owner.reshape(1, items_dev), tokens, norm_attn,
            w_query, w_key, w_value, wide_count, capacity,
        )

    def encode(pack, projected, tokens):
        return attend(pack, projected, tokens, w_output, norm_ffn)

    if wide_count == 16 and packs == 2:
        acc, other, slots_of = overlapped(w_input, w_down, tokens, encode_first, encode, sibling)
    else:
        projected = encode_first(tokens)
        slots_of = projected[5]
        normed, pooled = zip(*[encode(p, projected, tokens) for p in range(packs)])
        held = gather_any(w_input, w_down, wide_count)
        every = slice(0, held[0].shape[0])
        normed = (normed, [sibling(n) for n in normed])
        acc = feed(projected[4], normed, held, [(0, every, 1, every)], (pooled, []))
        acc, other = acc[0], sibling(acc[1])

    item_embed, send = pl.pallas_call(
        place_kernel,
        out_shape=(
            jax.ShapeDtypeStruct((items_dev, width), BF16),
            jax.ShapeDtypeStruct((slots, width + 128), BF16),
        ),
        compiler_params=params(),
        name="place",
    )(acc, other, norm_final, slots_of, cluster_slot[None])
    send = send.reshape(wide_count, capacity, width + 128)
    rows = lax.all_to_all(send, "wide", split_axis=0, concat_axis=0, tiled=True)
    codes = pl.pallas_call(
        code_kernel,
        out_shape=jax.ShapeDtypeStruct((slots, codes_count), BF16),
        compiler_params=params(),
        name="codes",
    )(rows.reshape(slots, width + 128), coarse, centroids)
    codes = codes.reshape(wide_count, capacity, codes_count)
    returned = lax.all_to_all(codes, "wide", split_axis=0, concat_axis=0, tiled=True)
    taking = (slots_of[0][:, None] == jnp.arange(slots, dtype=jnp.int32)[None, :]).astype(BF16)
    item_codes = jnp.dot(taking, returned.reshape(slots, codes_count), preferred_element_type=F32)
    return (item_embed, item_codes)


def solution(mesh):
    return jax.shard_map(
        local,
        mesh=mesh,
        in_specs=(
            P(("groups", "wide"), None, None),
            P(("groups", "wide"), None),
            P(),
            P(),
            P(),
            P(),
            P("wide", None),
            P("wide", None),
            P(),
            P(),
            P(),
            P(("groups", "wide"), None),
            P(("groups", "wide")),
            P("wide", None),
            P("wide", None, None),
        ),
        out_specs=(P(("groups", "wide"), None), P(("groups", "wide"), None)),
        check_vma=False,
    )
```

```python
import functools

import jax
import jax.numpy as jnp
from jax import lax
from jax.experimental import pallas as pl
from jax.experimental.pallas import tpu as pltpu
from jax.sharding import PartitionSpec as P

HEADS = 12
EPS = 1e-06
VMEM_BYTES = 16 * 1024 * 1024
F32 = jnp.float32
BF16 = jnp.bfloat16


def params():
    return pltpu.CompilerParams(vmem_limit_bytes=VMEM_BYTES)


def cost():
    return pl.CostEstimate(flops=2000000000, bytes_accessed=5000000, transcendentals=0)


def dot(a, b):
    return jnp.dot(a, b, preferred_element_type=F32)


def dot_nt(a, b):
    return lax.dot_general(a, b, (((1,), (1,)), ((), ())), preferred_element_type=F32)


def rms(values, gain):
    mean_sq = jnp.mean(values * values, axis=-1, keepdims=True)
    return values * lax.rsqrt(mean_sq + EPS) * gain


def item_rows(lengths, seq):
    items = lengths.shape[1]
    tri = (
        lax.broadcasted_iota(jnp.int32, (items, items), 0)
        <= lax.broadcasted_iota(jnp.int32, (items, items), 1)
    ).astype(F32)
    rows = jnp.broadcast_to(lengths.astype(F32), (8, items))
    ends = dot(rows.astype(BF16), tri.astype(BF16))[:1]
    starts = ends - rows[:1]
    place = lax.broadcasted_iota(jnp.int32, (seq, items), 0).astype(F32)
    return jnp.where((place < ends) & (place >= starts), 1.0, 0.0).astype(BF16)


def item_columns(lengths, seq):
    items = lengths.shape[1]
    row = lax.broadcasted_iota(jnp.int32, (items, items), 0)
    column = lax.broadcasted_iota(jnp.int32, (items, items), 1)
    rows = jnp.broadcast_to(lengths.astype(F32), (8, items)).astype(BF16)
    ends = dot_nt((column <= row).astype(F32).astype(BF16), rows)[:, :1]
    starts = dot_nt((column < row).astype(F32).astype(BF16), rows)[:, :1]
    place = lax.broadcasted_iota(jnp.int32, (items, seq), 1).astype(F32)
    return jnp.where((place < ends) & (place >= starts), 1.0, 0.0).astype(BF16)


def in_hbm(*arrays):
    return [pltpu.with_memory_space_constraint(a, pltpu.HBM) for a in arrays]


def project_kernel(
    other_ref, lengths_hbm, owner_hbm, gain_hbm, x_hbm, wq_hbm, wk_hbm, wv_hbm,
    q_ref, k_ref, v_ref, rows_ref, columns_ref, slot_ref,
    lengths_ref, owner_ref, gain_ref, x_ref, wq_ref, wk_ref, wv_ref, sems, *, wide, capacity,
):
    sources = (lengths_hbm, owner_hbm, gain_hbm, x_hbm, wq_hbm, wk_hbm, wv_hbm)
    here = (lengths_ref, owner_ref, gain_ref, x_ref, wq_ref, wk_ref, wv_ref)
    copies = [pltpu.make_async_copy(s, d, sems.at[i]) for i, (s, d) in enumerate(zip(sources, here))]
    for copy in copies:
        copy.start()
    for copy in copies[:3]:
        copy.wait()
    packs, seq, width = x_ref.shape
    per_pack = lengths_ref.shape[1]
    for pack in range(packs):
        rows_ref[pack * seq : (pack + 1) * seq] = item_rows(lengths_ref[pack : pack + 1], seq)
        for side, ref in enumerate((lengths_ref, other_ref)):
            at = (side * packs + pack) * per_pack
            columns_ref[at : at + per_pack] = item_columns(ref[pack : pack + 1], seq)
    owner = owner_ref[...]
    items = owner.shape[1]
    target = jnp.where(lax.broadcasted_iota(jnp.int32, (wide, items), 0) == owner, 1.0, 0.0)
    before = lax.broadcasted_iota(jnp.int32, (items, items), 0) < lax.broadcasted_iota(jnp.int32, (items, items), 1)
    earlier = dot(target.astype(BF16), jnp.where(before, 1.0, 0.0).astype(BF16))
    rank = jnp.sum(earlier * target, axis=0, keepdims=True)
    slot_ref[...] = owner * capacity + rank.astype(jnp.int32)
    gain = gain_ref[...][None]
    copies[3].wait()
    normed = [rms(x_ref[pack].astype(F32), gain).astype(BF16) for pack in range(packs)]
    normed = jnp.concatenate(normed, axis=0)
    for copy, w_ref, out_ref in zip(copies[4:], (wq_ref, wk_ref, wv_ref), (q_ref, k_ref, v_ref)):
        copy.wait()
        out_ref[...] = dot(normed, w_ref[...]).astype(BF16)


def project(lengths, other, owner, x, gain, wq, wk, wv, wide, capacity):
    packs, seq, width = x.shape
    items = lengths.shape[1]
    sources = (lengths, owner, gain, x, wq, wk, wv)
    return pl.pallas_call(
        functools.partial(project_kernel, wide=wide, capacity=capacity),
        in_specs=[pl.BlockSpec(memory_space=pltpu.VMEM)] + [pl.BlockSpec(memory_space=pltpu.HBM)] * len(sources),
        out_shape=(
            jax.ShapeDtypeStruct((packs * seq, width), BF16),
            jax.ShapeDtypeStruct((packs * seq, width), BF16),
            jax.ShapeDtypeStruct((packs * seq, width), BF16),
            jax.ShapeDtypeStruct((packs * seq, items), BF16),
            jax.ShapeDtypeStruct((2 * packs * items, seq), BF16),
            jax.ShapeDtypeStruct(owner.shape, jnp.int32),
        ),
        scratch_shapes=[pltpu.VMEM(a.shape, a.dtype) for a in sources]
        + [pltpu.SemaphoreType.DMA((len(sources),))],
        compiler_params=params(),
        cost_estimate=cost(),
        name="project",
    )(other, *in_hbm(*sources))


def hold_kernel(common, group_ref, w_in_hbm, w_down_hbm, held_ref, sems):
    half = (w_in_hbm.shape[0] - common) // 2
    start = pl.multiple_of(common + group_ref[0, 0] * half, 16)
    copies, at = [], 0
    for first, size in ((0, common), (start, half)):
        for source in (w_in_hbm, w_down_hbm):
            copies.append(
                pltpu.make_async_copy(source.at[pl.ds(first, size)], held_ref.at[pl.ds(at, size)], sems.at[len(copies)])
            )
            at += size
    for copy in copies:
        copy.start()
    for copy in copies:
        copy.wait()


def hold(w_input, w_down, common):
    rows, width = w_input.shape
    far = pl.BlockSpec(memory_space=pltpu.HBM)
    return pl.pallas_call(
        functools.partial(hold_kernel, common),
        in_specs=[pl.BlockSpec(memory_space=pltpu.SMEM), far, far],
        out_shape=jax.ShapeDtypeStruct((rows + common, width), BF16),
        scratch_shapes=[pltpu.SemaphoreType.DMA((4,))],
        compiler_params=params(),
        cost_estimate=cost(),
        name="hold",
    )(lax.axis_index("groups").astype(jnp.int32).reshape(1, 1), *in_hbm(w_input, w_down))


def attend_kernel(
    pack, q_ref, k_ref, v_ref, rows_ref, columns_ref, x_ref, wo_ref, gain_ref,
    normed2_ref, pooled_ref, ctx_ref,
):
    _, seq, width = x_ref.shape
    items = rows_ref.shape[1]
    head = width // HEADS
    base = pack * seq
    onehot = rows_ref[base : base + seq]
    block, window, lanes = 64, 128, 256
    heads = lanes // head
    lane_head = lax.broadcasted_iota(jnp.int32, (block, lanes), 1) // head
    for start in range(0, seq, block):
        first = min(max(start - (window - block) // 2, 0), seq - window)
        same = dot_nt(onehot[start : start + block], onehot[first : first + window])
        same = jnp.concatenate([same] * heads, axis=0) > 0.5
        keys = slice(base + first, base + first + window)
        for column in range(0, width, lanes):
            across = slice(column, column + lanes)
            query = q_ref[base + start : base + start + block, across]
            stacked = jnp.concatenate(
                [jnp.where(lane_head == h, query, jnp.zeros_like(query)) for h in range(heads)], axis=0
            )
            scores = jnp.where(same, dot_nt(stacked, k_ref[keys, across]), -1e30)
            expo = jnp.exp(scores - jnp.max(scores, axis=-1, keepdims=True))
            probs = (expo * (1.0 / jnp.sum(expo, axis=-1, keepdims=True))).astype(BF16)
            mixed = dot(probs, v_ref[keys, across])
            context = mixed[:block]
            for h in range(1, heads):
                context = jnp.where(lane_head == h, mixed[h * block : (h + 1) * block], context)
            ctx_ref[start : start + block, across] = context.astype(BF16)
    stream = (x_ref[pack].astype(F32) + dot(ctx_ref[...], wo_ref[...])).astype(BF16)
    normed2_ref[...] = rms(stream.astype(F32), gain_ref[...][None]).astype(BF16)
    pooled_ref[...] = dot(columns_ref[pack * items : (pack + 1) * items], stream)


def attend(pack, projected, x, wo, gain2):
    _, seq, width = x.shape
    items = projected[3].shape[1]
    return pl.pallas_call(
        functools.partial(attend_kernel, pack),
        out_shape=(
            jax.ShapeDtypeStruct((seq, width), BF16),
            jax.ShapeDtypeStruct((items, width), F32),
        ),
        scratch_shapes=[pltpu.VMEM((seq, width), BF16)],
        compiler_params=params(),
        cost_estimate=cost(),
        name="attend",
    )(*projected[:5], x, wo, gain2)


def feed_side_kernel(side, n_held, pieces, columns_ref, *refs):
    normed_refs, held, (base_ref, out_ref) = refs[: -2 - n_held], refs[-2 - n_held : -2], refs[-2:]
    w_in = jnp.concatenate([held[i][r] for i, r, _, _ in pieces], axis=0)
    w_down = jnp.concatenate([held[i][r] for _, _, i, r in pieces], axis=0)
    packs = len(normed_refs)
    items = columns_ref.shape[0] // (2 * packs)
    pooled = []
    for pack in range(packs):
        hidden = jnp.maximum(dot_nt(normed_refs[pack][...], w_in), 0.0).astype(BF16)
        at = (side * packs + pack) * items
        pooled.append(dot(columns_ref[at : at + items], hidden).astype(BF16))
    out_ref[...] = base_ref[...] + dot(jnp.concatenate(pooled, axis=0), w_down)


def feed_side(side, columns, normed, held, pieces, base):
    return pl.pallas_call(
        functools.partial(feed_side_kernel, side, len(held), pieces),
        out_shape=jax.ShapeDtypeStruct(base.shape, F32),
        compiler_params=params(),
        cost_estimate=cost(),
        name="feed_side",
    )(columns, *normed[side], *held, base)


def feed_kernel(n_normed, n_held, pieces, n_base, columns_ref, *refs):
    normed_refs, refs = (refs[:n_normed], refs[n_normed : 2 * n_normed]), refs[2 * n_normed :]
    held, refs = refs[:n_held], refs[n_held:]
    bases, outs = (refs[: n_base[0]], refs[n_base[0] : sum(n_base)]), refs[sum(n_base) :]
    w_in = jnp.concatenate([held[i][r] for i, r, _, _ in pieces], axis=0)
    w_down = jnp.concatenate([held[i][r] for _, _, i, r in pieces], axis=0)
    packs = n_normed
    items = columns_ref.shape[0] // (2 * packs)
    for side in range(2):
        pooled = []
        for pack in range(packs):
            hidden = jnp.maximum(dot_nt(normed_refs[side][pack][...], w_in), 0.0).astype(BF16)
            at = (side * packs + pack) * items
            pooled.append(dot(columns_ref[at : at + items], hidden).astype(BF16))
        part = dot(jnp.concatenate(pooled, axis=0), w_down)
        if bases[side]:
            part = part + jnp.concatenate([r[...] for r in bases[side]], axis=0)
        outs[side][...] = part


def feed(columns, normed, held, pieces, bases):
    items = columns.shape[0] // 2
    width = held[0].shape[1]
    n_base = tuple(len(b) for b in bases)
    return pl.pallas_call(
        functools.partial(feed_kernel, len(normed[0]), len(held), pieces, n_base),
        out_shape=(jax.ShapeDtypeStruct((items, width), F32),) * 2,
        compiler_params=params(),
        cost_estimate=cost(),
        name="feed",
    )(columns, *normed[0], *normed[1], *held, *bases[0], *bases[1])


def place_kernel(acc_ref, other_ref, gain_ref, slot_ref, cluster_ref, embed_ref, send_ref):
    width = embed_ref.shape[1]
    embed = rms(acc_ref[...] + other_ref[...], gain_ref[...][None]).astype(BF16)
    embed_ref[...] = embed
    slots, items = send_ref.shape[0], embed.shape[0]
    placing = jnp.where(
        lax.broadcasted_iota(jnp.int32, (slots, items), 0) == slot_ref[...], 1.0, 0.0
    ).astype(BF16)
    send_ref[:, :width] = dot(placing, embed).astype(BF16)
    clusters = send_ref.shape[1] - width
    chosen = jnp.where(
        lax.broadcasted_iota(jnp.int32, (clusters, items), 0) == cluster_ref[...], 1.0, 0.0
    ).astype(BF16)
    send_ref[:, width:] = dot_nt(placing, chosen).astype(BF16)


def code_kernel(rows_ref, coarse_ref, books_ref, out_ref):
    clusters, codes, width = books_ref.shape
    slots = rows_ref.shape[0]
    spare = -clusters % 16
    coarse = jnp.concatenate([coarse_ref[...], jnp.zeros((spare, width), BF16)], axis=0)
    rows = jnp.concatenate([rows_ref[:, :width], coarse], axis=0)
    total = jnp.zeros((slots, codes), F32)
    for cluster in range(clusters):
        direct = dot_nt(rows, books_ref[cluster])
        offset = direct[slots + cluster : slots + cluster + 1]
        chosen = rows_ref[:, width + cluster : width + cluster + 1].astype(F32)
        total = total + (direct[:slots] - offset) * chosen
    out_ref[...] = total.astype(BF16)


def flip(axis_name, count, bits):
    pairs = [(i, i ^ bits) for i in range(count)]
    return lambda value: lax.ppermute(value, axis_name, pairs)


def gather_any(w_input, w_down, count):
    groups = [list(range(core, count, 2)) for core in range(2)]
    w_in = lax.all_gather(w_input, "wide", axis=0, tiled=True, axis_index_groups=groups)
    down = lax.all_gather(w_down, "wide", axis=0, tiled=True, axis_index_groups=groups)
    return w_in, down


def overlapped(w_input, w_down, tokens, encode_first, encode, sibling):
    rows = w_input.shape[0]
    common = rows // 3 // 16 * 16
    half = (rows - common) // 2
    split, both, every = 2 * common, 2 * half, 2 * (common + half)
    near, side, twin = flip("wide", 16, 4), flip("wide", 16, 2), flip("groups", 2, 1)
    line = lax.axis_index("wide") // 4
    inner = (line == 1) | (line == 2)

    def along(value, hops):
        pairs = [(4 * a + i, 4 * b + i) for a, b in hops for i in range(4)]
        return lax.ppermute(value, "wide", pairs)

    def amid(value):
        pairs = [(i, i ^ 12 if i // 4 in (1, 2) else i ^ 1) for i in range(16)]
        return lax.ppermute(value, "wide", pairs)

    after = lax.optimization_barrier

    def blocks(i):
        return [
            (i, slice(0, common), i, slice(common, split)),
            (i, slice(split, split + half), i, slice(split + half, every)),
        ]

    def rest(i, at=0):
        return [(i, slice(at, at + half), i, slice(at + half, at + both))]

    def cat(a, b):
        return jnp.concatenate([a, b], axis=0)

    held = hold(w_input, w_down, common)
    middle, near1, side0 = amid(held), near(held), side(held)
    projected = encode_first(tokens)
    side0, near1, middle, projected = after((side0, near1, middle, projected))
    columns = projected[4]

    side1 = side(near1)
    far2 = along(jnp.where(inner, middle, held), [(1, 0), (0, 2), (2, 3), (3, 1)])
    x0 = twin(cat(side0[split:], near1[split:]))
    first = encode(0, projected, tokens)
    side1, far2, first, projected = after((side1, far2, first, projected))

    side2, outer = side(far2), near(far2)
    x0, projected = after((x0, projected))
    x1 = twin(cat(side1[split:], far2[split:]))
    last_inner = amid(x0[:both])
    second = encode(1, projected, tokens)
    side2, x1, outer, last_inner, second = after((side2, x1, outer, last_inner, second))

    far3 = jnp.where(inner, middle, outer)
    side3, x2 = side(far3), twin(cat(side2[split:], far3[split:]))
    last_outer = along(x1[:both], [(2, 0), (0, 1), (1, 3), (3, 2)])
    normed = ((first[0], second[0]), (sibling(first[0]), sibling(second[0])))
    own = [(0, slice(0, rows), 1, slice(0, rows))]
    pieces = own + blocks(2) + rest(3) + blocks(4) + rest(3, both) + blocks(5) + rest(6)
    acc = feed(columns, normed, [w_input, w_down, side0, x0, near1, side1, x1], pieces, ([first[1], second[1]], []))
    pieces = blocks(0) + rest(1, both) + blocks(2) + blocks(3)
    acc = feed(columns, normed, [far2, x1, side2, far3], pieces, ([acc[0]], [acc[1]]))
    side3, x2, last_outer, acc = after((side3, x2, last_outer, acc))

    last = jnp.where(inner, last_inner, last_outer)
    pieces = rest(0) + rest(0, both) + blocks(1) + rest(2)
    held = [x2, side3, last]
    there = sibling(feed_side(1, columns, normed, held, pieces, acc[1]))
    return feed_side(0, columns, normed, held, pieces, acc[0]), there, projected[5]


def local(
    tokens, item_lengths, w_query, w_key, w_value, w_output, w_input, w_down,
    norm_attn, norm_ffn, norm_final, owner, cluster_slot, coarse, centroids,
):
    packs, seq, width = tokens.shape
    per_pack = item_lengths.shape[1]
    wide_count = lax.axis_size("wide")
    items_dev = packs * per_pack
    capacity = max(2, 2 * items_dev // wide_count)
    slots = wide_count * capacity
    local_clusters, codes_count, _ = centroids.shape
    sibling = flip("wide", wide_count, 1)

    other_lengths = sibling(item_lengths)

    def encode_first(tokens):
        return project(
            item_lengths, other_lengths, owner.reshape(1, items_dev), tokens, norm_attn,
            w_query, w_key, w_value, wide_count, capacity,
        )

    def encode(pack, projected, tokens):
        return attend(pack, projected, tokens, w_output, norm_ffn)

    if wide_count == 16 and packs == 2:
        acc, other, slots_of = overlapped(w_input, w_down, tokens, encode_first, encode, sibling)
    else:
        projected = encode_first(tokens)
        slots_of = projected[5]
        normed, pooled = zip(*[encode(p, projected, tokens) for p in range(packs)])
        held = gather_any(w_input, w_down, wide_count)
        every = slice(0, held[0].shape[0])
        normed = (normed, [sibling(n) for n in normed])
        acc = feed(projected[4], normed, held, [(0, every, 1, every)], (pooled, []))
        acc, other = acc[0], sibling(acc[1])

    item_embed, send = pl.pallas_call(
        place_kernel,
        out_shape=(
            jax.ShapeDtypeStruct((items_dev, width), BF16),
            jax.ShapeDtypeStruct((slots, width + 128), BF16),
        ),
        compiler_params=params(),
        name="place",
    )(acc, other, norm_final, slots_of, cluster_slot[None])
    send = send.reshape(wide_count, capacity, width + 128)
    rows = lax.all_to_all(send, "wide", split_axis=0, concat_axis=0, tiled=True)
    codes = pl.pallas_call(
        code_kernel,
        out_shape=jax.ShapeDtypeStruct((slots, codes_count), BF16),
        compiler_params=params(),
        name="codes",
    )(rows.reshape(slots, width + 128), coarse, centroids)
    codes = codes.reshape(wide_count, capacity, codes_count)
    returned = lax.all_to_all(codes, "wide", split_axis=0, concat_axis=0, tiled=True)
    taking = (slots_of[0][:, None] == jnp.arange(slots, dtype=jnp.int32)[None, :]).astype(BF16)
    item_codes = jnp.dot(taking, returned.reshape(slots, codes_count), preferred_element_type=F32)
    return (item_embed, item_codes)


def solution(mesh):
    return jax.shard_map(
        local,
        mesh=mesh,
        in_specs=(
            P(("groups", "wide"), None, None),
            P(("groups", "wide"), None),
            P(),
            P(),
            P(),
            P(),
            P("wide", None),
            P("wide", None),
            P(),
            P(),
            P(),
            P(("groups", "wide"), None),
            P(("groups", "wide")),
            P("wide", None),
            P("wide", None, None),
        ),
        out_specs=(P(("groups", "wide"), None), P(("groups", "wide"), None)),
        check_vma=False,
    )
```

```python
import functools

import jax
import jax.numpy as jnp
from jax import lax
from jax.experimental import pallas as pl
from jax.experimental.pallas import tpu as pltpu
from jax.sharding import PartitionSpec as P

HEADS = 12
EPS = 1e-06
VMEM_BYTES = 16 * 1024 * 1024
F32 = jnp.float32
BF16 = jnp.bfloat16


def params():
    return pltpu.CompilerParams(vmem_limit_bytes=VMEM_BYTES)


def cost():
    return pl.CostEstimate(flops=2000000000, bytes_accessed=5000000, transcendentals=0)


def dot(a, b):
    return jnp.dot(a, b, preferred_element_type=F32)


def dot_nt(a, b):
    return lax.dot_general(a, b, (((1,), (1,)), ((), ())), preferred_element_type=F32)


def rms(values, gain):
    mean_sq = jnp.mean(values * values, axis=-1, keepdims=True)
    return values * lax.rsqrt(mean_sq + EPS) * gain


def item_rows(lengths, seq):
    items = lengths.shape[1]
    tri = (
        lax.broadcasted_iota(jnp.int32, (items, items), 0)
        <= lax.broadcasted_iota(jnp.int32, (items, items), 1)
    ).astype(F32)
    rows = jnp.broadcast_to(lengths.astype(F32), (8, items))
    ends = dot(rows.astype(BF16), tri.astype(BF16))[:1]
    starts = ends - rows[:1]
    place = lax.broadcasted_iota(jnp.int32, (seq, items), 0).astype(F32)
    return jnp.where((place < ends) & (place >= starts), 1.0, 0.0).astype(BF16)


def item_columns(lengths, seq):
    items = lengths.shape[1]
    row = lax.broadcasted_iota(jnp.int32, (items, items), 0)
    column = lax.broadcasted_iota(jnp.int32, (items, items), 1)
    rows = jnp.broadcast_to(lengths.astype(F32), (8, items)).astype(BF16)
    ends = dot_nt((column <= row).astype(F32).astype(BF16), rows)[:, :1]
    starts = dot_nt((column < row).astype(F32).astype(BF16), rows)[:, :1]
    place = lax.broadcasted_iota(jnp.int32, (items, seq), 1).astype(F32)
    return jnp.where((place < ends) & (place >= starts), 1.0, 0.0).astype(BF16)


def in_hbm(*arrays):
    return [pltpu.with_memory_space_constraint(a, pltpu.HBM) for a in arrays]


def project_kernel(
    other_ref, lengths_hbm, owner_hbm, gain_hbm, x_hbm, wq_hbm, wk_hbm, wv_hbm,
    q_ref, k_ref, v_ref, rows_ref, columns_ref, slot_ref,
    lengths_ref, owner_ref, gain_ref, x_ref, wq_ref, wk_ref, wv_ref, sems, *, wide, capacity,
):
    sources = (lengths_hbm, owner_hbm, gain_hbm, x_hbm, wq_hbm, wk_hbm, wv_hbm)
    here = (lengths_ref, owner_ref, gain_ref, x_ref, wq_ref, wk_ref, wv_ref)
    copies = [pltpu.make_async_copy(s, d, sems.at[i]) for i, (s, d) in enumerate(zip(sources, here))]
    for copy in copies:
        copy.start()
    for copy in copies[:3]:
        copy.wait()
    packs, seq, width = x_ref.shape
    per_pack = lengths_ref.shape[1]
    for pack in range(packs):
        rows_ref[pack * seq : (pack + 1) * seq] = item_rows(lengths_ref[pack : pack + 1], seq)
        for side, ref in enumerate((lengths_ref, other_ref)):
            at = (side * packs + pack) * per_pack
            columns_ref[at : at + per_pack] = item_columns(ref[pack : pack + 1], seq)
    owner = owner_ref[...]
    items = owner.shape[1]
    target = jnp.where(lax.broadcasted_iota(jnp.int32, (wide, items), 0) == owner, 1.0, 0.0)
    before = lax.broadcasted_iota(jnp.int32, (items, items), 0) < lax.broadcasted_iota(jnp.int32, (items, items), 1)
    earlier = dot(target.astype(BF16), jnp.where(before, 1.0, 0.0).astype(BF16))
    rank = jnp.sum(earlier * target, axis=0, keepdims=True)
    slot_ref[...] = owner * capacity + rank.astype(jnp.int32)
    gain = gain_ref[...][None]
    copies[3].wait()
    normed = [rms(x_ref[pack].astype(F32), gain).astype(BF16) for pack in range(packs)]
    normed = jnp.concatenate(normed, axis=0)
    for copy, w_ref, out_ref in zip(copies[4:], (wq_ref, wk_ref, wv_ref), (q_ref, k_ref, v_ref)):
        copy.wait()
        out_ref[...] = dot(normed, w_ref[...]).astype(BF16)


def project(lengths, other, owner, x, gain, wq, wk, wv, wide, capacity):
    packs, seq, width = x.shape
    items = lengths.shape[1]
    sources = (lengths, owner, gain, x, wq, wk, wv)
    return pl.pallas_call(
        functools.partial(project_kernel, wide=wide, capacity=capacity),
        in_specs=[pl.BlockSpec(memory_space=pltpu.VMEM)] + [pl.BlockSpec(memory_space=pltpu.HBM)] * len(sources),
        out_shape=(
            jax.ShapeDtypeStruct((packs * seq, width), BF16),
            jax.ShapeDtypeStruct((packs * seq, width), BF16),
            jax.ShapeDtypeStruct((packs * seq, width), BF16),
            jax.ShapeDtypeStruct((packs * seq, items), BF16),
            jax.ShapeDtypeStruct((2 * packs * items, seq), BF16),
            jax.ShapeDtypeStruct(owner.shape, jnp.int32),
        ),
        scratch_shapes=[pltpu.VMEM(a.shape, a.dtype) for a in sources]
        + [pltpu.SemaphoreType.DMA((len(sources),))],
        compiler_params=params(),
        cost_estimate=cost(),
        name="project",
    )(other, *in_hbm(*sources))


def hold_kernel(common, group_ref, w_in_hbm, w_down_hbm, held_ref, sems):
    half = (w_in_hbm.shape[0] - common) // 2
    start = pl.multiple_of(common + group_ref[0, 0] * half, 16)
    copies, at = [], 0
    for first, size in ((0, common), (start, half)):
        for source in (w_in_hbm, w_down_hbm):
            copies.append(
                pltpu.make_async_copy(source.at[pl.ds(first, size)], held_ref.at[pl.ds(at, size)], sems.at[len(copies)])
            )
            at += size
    for copy in copies:
        copy.start()
    for copy in copies:
        copy.wait()


def hold(w_input, w_down, common):
    rows, width = w_input.shape
    far = pl.BlockSpec(memory_space=pltpu.HBM)
    return pl.pallas_call(
        functools.partial(hold_kernel, common),
        in_specs=[pl.BlockSpec(memory_space=pltpu.SMEM), far, far],
        out_shape=jax.ShapeDtypeStruct((rows + common, width), BF16),
        scratch_shapes=[pltpu.SemaphoreType.DMA((4,))],
        compiler_params=params(),
        cost_estimate=cost(),
        name="hold",
    )(lax.axis_index("groups").astype(jnp.int32).reshape(1, 1), *in_hbm(w_input, w_down))


def attend_kernel(
    pack, q_ref, k_ref, v_ref, rows_ref, columns_ref, x_ref, wo_ref, gain_ref,
    normed2_ref, pooled_ref, ctx_ref,
):
    _, seq, width = x_ref.shape
    items = rows_ref.shape[1]
    head = width // HEADS
    base = pack * seq
    onehot = rows_ref[base : base + seq]
    block, window, lanes = 64, 128, 256
    heads = lanes // head
    lane_head = lax.broadcasted_iota(jnp.int32, (block, lanes), 1) // head
    for start in range(0, seq, block):
        first = min(max(start - (window - block) // 2, 0), seq - window)
        same = dot_nt(onehot[start : start + block], onehot[first : first + window])
        same = jnp.concatenate([same] * heads, axis=0) > 0.5
        keys = slice(base + first, base + first + window)
        for column in range(0, width, lanes):
            across = slice(column, column + lanes)
            query = q_ref[base + start : base + start + block, across]
            stacked = jnp.concatenate(
                [jnp.where(lane_head == h, query, jnp.zeros_like(query)) for h in range(heads)], axis=0
            )
            scores = jnp.where(same, dot_nt(stacked, k_ref[keys, across]), -1e30)
            expo = jnp.exp(scores - jnp.max(scores, axis=-1, keepdims=True))
            probs = (expo * (1.0 / jnp.sum(expo, axis=-1, keepdims=True))).astype(BF16)
            mixed = dot(probs, v_ref[keys, across])
            context = mixed[:block]
            for h in range(1, heads):
                context = jnp.where(lane_head == h, mixed[h * block : (h + 1) * block], context)
            ctx_ref[start : start + block, across] = context.astype(BF16)
    stream = (x_ref[pack].astype(F32) + dot(ctx_ref[...], wo_ref[...])).astype(BF16)
    normed2_ref[...] = rms(stream.astype(F32), gain_ref[...][None]).astype(BF16)
    pooled_ref[...] = dot(columns_ref[pack * items : (pack + 1) * items], stream)


def attend(pack, projected, x, wo, gain2):
    _, seq, width = x.shape
    items = projected[3].shape[1]
    return pl.pallas_call(
        functools.partial(attend_kernel, pack),
        out_shape=(
            jax.ShapeDtypeStruct((seq, width), BF16),
            jax.ShapeDtypeStruct((items, width), F32),
        ),
        scratch_shapes=[pltpu.VMEM((seq, width), BF16)],
        compiler_params=params(),
        cost_estimate=cost(),
        name="attend",
    )(*projected[:5], x, wo, gain2)


def feed_side_kernel(side, n_held, pieces, columns_ref, *refs):
    normed_refs, held, (base_ref, out_ref) = refs[: -2 - n_held], refs[-2 - n_held : -2], refs[-2:]
    w_in = jnp.concatenate([held[i][r] for i, r, _, _ in pieces], axis=0)
    w_down = jnp.concatenate([held[i][r] for _, _, i, r in pieces], axis=0)
    packs = len(normed_refs)
    items = columns_ref.shape[0] // (2 * packs)
    pooled = []
    for pack in range(packs):
        hidden = jnp.maximum(dot_nt(normed_refs[pack][...], w_in), 0.0).astype(BF16)
        at = (side * packs + pack) * items
        pooled.append(dot(columns_ref[at : at + items], hidden).astype(BF16))
    total = base_ref[...] + dot(jnp.concatenate(pooled, axis=0), w_down)
    out_ref[...] = total.astype(out_ref.dtype)


def feed_side(side, columns, normed, held, pieces, base, dtype=F32):
    return pl.pallas_call(
        functools.partial(feed_side_kernel, side, len(held), pieces),
        out_shape=jax.ShapeDtypeStruct(base.shape, dtype),
        compiler_params=params(),
        cost_estimate=cost(),
        name="feed_side",
    )(columns, *normed[side], *held, base)


def feed_kernel(n_normed, n_held, pieces, n_base, columns_ref, *refs):
    normed_refs, refs = (refs[:n_normed], refs[n_normed : 2 * n_normed]), refs[2 * n_normed :]
    held, refs = refs[:n_held], refs[n_held:]
    bases, outs = (refs[: n_base[0]], refs[n_base[0] : sum(n_base)]), refs[sum(n_base) :]
    w_in = jnp.concatenate([held[i][r] for i, r, _, _ in pieces], axis=0)
    w_down = jnp.concatenate([held[i][r] for _, _, i, r in pieces], axis=0)
    packs = n_normed
    items = columns_ref.shape[0] // (2 * packs)
    for side in range(2):
        pooled = []
        for pack in range(packs):
            hidden = jnp.maximum(dot_nt(normed_refs[side][pack][...], w_in), 0.0).astype(BF16)
            at = (side * packs + pack) * items
            pooled.append(dot(columns_ref[at : at + items], hidden).astype(BF16))
        part = dot(jnp.concatenate(pooled, axis=0), w_down)
        if bases[side]:
            part = part + jnp.concatenate([r[...] for r in bases[side]], axis=0)
        outs[side][...] = part


def feed(columns, normed, held, pieces, bases):
    items = columns.shape[0] // 2
    width = held[0].shape[1]
    n_base = tuple(len(b) for b in bases)
    return pl.pallas_call(
        functools.partial(feed_kernel, len(normed[0]), len(held), pieces, n_base),
        out_shape=(jax.ShapeDtypeStruct((items, width), F32),) * 2,
        compiler_params=params(),
        cost_estimate=cost(),
        name="feed",
    )(columns, *normed[0], *normed[1], *held, *bases[0], *bases[1])


def place_kernel(acc_ref, other_ref, gain_ref, slot_ref, cluster_ref, embed_ref, send_ref):
    width = embed_ref.shape[1]
    embed = rms(acc_ref[...] + other_ref[...].astype(F32), gain_ref[...][None]).astype(BF16)
    embed_ref[...] = embed
    slots, items = send_ref.shape[0], embed.shape[0]
    placing = jnp.where(
        lax.broadcasted_iota(jnp.int32, (slots, items), 0) == slot_ref[...], 1.0, 0.0
    ).astype(BF16)
    send_ref[:, :width] = dot(placing, embed).astype(BF16)
    clusters = send_ref.shape[1] - width
    chosen = jnp.where(
        lax.broadcasted_iota(jnp.int32, (clusters, items), 0) == cluster_ref[...], 1.0, 0.0
    ).astype(BF16)
    send_ref[:, width:] = dot_nt(placing, chosen).astype(BF16)


def code_kernel(rows_ref, coarse_ref, books_ref, out_ref):
    clusters, codes, width = books_ref.shape
    slots = rows_ref.shape[0]
    spare = -clusters % 16
    coarse = jnp.concatenate([coarse_ref[...], jnp.zeros((spare, width), BF16)], axis=0)
    rows = jnp.concatenate([rows_ref[:, :width], coarse], axis=0)
    total = jnp.zeros((slots, codes), F32)
    for cluster in range(clusters):
        direct = dot_nt(rows, books_ref[cluster])
        offset = direct[slots + cluster : slots + cluster + 1]
        chosen = rows_ref[:, width + cluster : width + cluster + 1].astype(F32)
        total = total + (direct[:slots] - offset) * chosen
    out_ref[...] = total.astype(BF16)


def flip(axis_name, count, bits):
    pairs = [(i, i ^ bits) for i in range(count)]
    return lambda value: lax.ppermute(value, axis_name, pairs)


def gather_any(w_input, w_down, count):
    groups = [list(range(core, count, 2)) for core in range(2)]
    w_in = lax.all_gather(w_input, "wide", axis=0, tiled=True, axis_index_groups=groups)
    down = lax.all_gather(w_down, "wide", axis=0, tiled=True, axis_index_groups=groups)
    return w_in, down


def overlapped(w_input, w_down, tokens, encode_first, encode, sibling):
    rows = w_input.shape[0]
    common = rows // 3 // 16 * 16
    half = (rows - common) // 2
    split, both, every = 2 * common, 2 * half, 2 * (common + half)
    near, side, twin = flip("wide", 16, 4), flip("wide", 16, 2), flip("groups", 2, 1)
    line = lax.axis_index("wide") // 4
    inner = (line == 1) | (line == 2)

    def along(value, hops):
        pairs = [(4 * a + i, 4 * b + i) for a, b in hops for i in range(4)]
        return lax.ppermute(value, "wide", pairs)

    def amid(value):
        pairs = [(i, i ^ 12 if i // 4 in (1, 2) else i ^ 1) for i in range(16)]
        return lax.ppermute(value, "wide", pairs)

    after = lax.optimization_barrier

    def blocks(i):
        return [
            (i, slice(0, common), i, slice(common, split)),
            (i, slice(split, split + half), i, slice(split + half, every)),
        ]

    def rest(i, at=0):
        return [(i, slice(at, at + half), i, slice(at + half, at + both))]

    def cat(a, b):
        return jnp.concatenate([a, b], axis=0)

    held = hold(w_input, w_down, common)
    middle, near1, side0 = amid(held), near(held), side(held)
    projected = encode_first(tokens)
    side0, near1, middle, projected = after((side0, near1, middle, projected))
    columns = projected[4]

    far2 = along(jnp.where(inner, middle, held), [(1, 0), (0, 2), (2, 3), (3, 1)])
    x0 = twin(cat(side0[split:], near1[split:]))
    side1 = side(near1)
    first = encode(0, projected, tokens)
    side1, far2, first, projected = after((side1, far2, first, projected))

    side2, outer = side(far2), near(far2)
    x0, projected = after((x0, projected))
    x1 = twin(cat(side1[split:], far2[split:]))
    last_inner = amid(x0[:both])
    second = encode(1, projected, tokens)
    side2, x1, outer, last_inner, second = after((side2, x1, outer, last_inner, second))

    far3 = jnp.where(inner, middle, outer)
    side3, x2 = side(far3), twin(cat(side2[split:], far3[split:]))
    last_outer = along(x1[:both], [(2, 0), (0, 1), (1, 3), (3, 2)])
    normed = ((first[0], second[0]), (sibling(first[0]), sibling(second[0])))
    own = [(0, slice(0, rows), 1, slice(0, rows))]
    pieces = own + blocks(2) + rest(3) + blocks(4) + rest(3, both) + blocks(5) + rest(6)
    acc = feed(columns, normed, [w_input, w_down, side0, x0, near1, side1, x1], pieces, ([first[1], second[1]], []))
    pieces = blocks(0) + rest(1, both) + blocks(2) + blocks(3)
    acc = feed(columns, normed, [far2, x1, side2, far3], pieces, ([acc[0]], [acc[1]]))
    side3, x2, last_outer, acc = after((side3, x2, last_outer, acc))

    last = jnp.where(inner, last_inner, last_outer)
    pieces = rest(0) + rest(0, both) + blocks(1) + rest(2)
    held = [x2, side3, last]
    there = sibling(feed_side(1, columns, normed, held, pieces, acc[1], BF16))
    return feed_side(0, columns, normed, held, pieces, acc[0]), there, projected[5]


def local(
    tokens, item_lengths, w_query, w_key, w_value, w_output, w_input, w_down,
    norm_attn, norm_ffn, norm_final, owner, cluster_slot, coarse, centroids,
):
    packs, seq, width = tokens.shape
    per_pack = item_lengths.shape[1]
    wide_count = lax.axis_size("wide")
    items_dev = packs * per_pack
    capacity = max(2, 2 * items_dev // wide_count)
    slots = wide_count * capacity
    local_clusters, codes_count, _ = centroids.shape
    sibling = flip("wide", wide_count, 1)

    other_lengths = sibling(item_lengths)

    def encode_first(tokens):
        return project(
            item_lengths, other_lengths, owner.reshape(1, items_dev), tokens, norm_attn,
            w_query, w_key, w_value, wide_count, capacity,
        )

    def encode(pack, projected, tokens):
        return attend(pack, projected, tokens, w_output, norm_ffn)

    if wide_count == 16 and packs == 2:
        acc, other, slots_of = overlapped(w_input, w_down, tokens, encode_first, encode, sibling)
    else:
        projected = encode_first(tokens)
        slots_of = projected[5]
        normed, pooled = zip(*[encode(p, projected, tokens) for p in range(packs)])
        held = gather_any(w_input, w_down, wide_count)
        every = slice(0, held[0].shape[0])
        normed = (normed, [sibling(n) for n in normed])
        acc = feed(projected[4], normed, held, [(0, every, 1, every)], (pooled, []))
        acc, other = acc[0], sibling(acc[1])

    item_embed, send = pl.pallas_call(
        place_kernel,
        out_shape=(
            jax.ShapeDtypeStruct((items_dev, width), BF16),
            jax.ShapeDtypeStruct((slots, width + 128), BF16),
        ),
        compiler_params=params(),
        name="place",
    )(acc, other, norm_final, slots_of, cluster_slot[None])
    send = send.reshape(wide_count, capacity, width + 128)
    rows = lax.all_to_all(send, "wide", split_axis=0, concat_axis=0, tiled=True)
    codes = pl.pallas_call(
        code_kernel,
        out_shape=jax.ShapeDtypeStruct((slots, codes_count), BF16),
        compiler_params=params(),
        name="codes",
    )(rows.reshape(slots, width + 128), coarse, centroids)
    codes = codes.reshape(wide_count, capacity, codes_count)
    returned = lax.all_to_all(codes, "wide", split_axis=0, concat_axis=0, tiled=True)
    taking = (slots_of[0][:, None] == jnp.arange(slots, dtype=jnp.int32)[None, :]).astype(BF16)
    item_codes = jnp.dot(taking, returned.reshape(slots, codes_count), preferred_element_type=F32)
    return (item_embed, item_codes)


def solution(mesh):
    return jax.shard_map(
        local,
        mesh=mesh,
        in_specs=(
            P(("groups", "wide"), None, None),
            P(("groups", "wide"), None),
            P(),
            P(),
            P(),
            P(),
            P("wide", None),
            P("wide", None),
            P(),
            P(),
            P(),
            P(("groups", "wide"), None),
            P(("groups", "wide")),
            P("wide", None),
            P("wide", None, None),
        ),
        out_specs=(P(("groups", "wide"), None), P(("groups", "wide"), None)),
        check_vma=False,
    )
```

```python
import functools

import jax
import jax.numpy as jnp
from jax import lax
from jax.experimental import pallas as pl
from jax.experimental.pallas import tpu as pltpu
from jax.sharding import PartitionSpec as P

HEADS = 12
EPS = 1e-06
VMEM_BYTES = 16 * 1024 * 1024
F32 = jnp.float32
BF16 = jnp.bfloat16


def params():
    return pltpu.CompilerParams(vmem_limit_bytes=VMEM_BYTES)


def cost():
    return pl.CostEstimate(flops=2000000000, bytes_accessed=5000000, transcendentals=0)


def dot(a, b):
    return jnp.dot(a, b, preferred_element_type=F32)


def dot_nt(a, b):
    return lax.dot_general(a, b, (((1,), (1,)), ((), ())), preferred_element_type=F32)


def rms(values, gain):
    mean_sq = jnp.mean(values * values, axis=-1, keepdims=True)
    return values * lax.rsqrt(mean_sq + EPS) * gain


def item_rows(lengths, seq):
    items = lengths.shape[1]
    tri = (
        lax.broadcasted_iota(jnp.int32, (items, items), 0)
        <= lax.broadcasted_iota(jnp.int32, (items, items), 1)
    ).astype(F32)
    rows = jnp.broadcast_to(lengths.astype(F32), (8, items))
    ends = dot(rows.astype(BF16), tri.astype(BF16))[:1]
    starts = ends - rows[:1]
    place = lax.broadcasted_iota(jnp.int32, (seq, items), 0).astype(F32)
    return jnp.where((place < ends) & (place >= starts), 1.0, 0.0).astype(BF16)


def item_columns(lengths, seq):
    items = lengths.shape[1]
    row = lax.broadcasted_iota(jnp.int32, (items, items), 0)
    column = lax.broadcasted_iota(jnp.int32, (items, items), 1)
    rows = jnp.broadcast_to(lengths.astype(F32), (8, items)).astype(BF16)
    ends = dot_nt((column <= row).astype(F32).astype(BF16), rows)[:, :1]
    starts = dot_nt((column < row).astype(F32).astype(BF16), rows)[:, :1]
    place = lax.broadcasted_iota(jnp.int32, (items, seq), 1).astype(F32)
    return jnp.where((place < ends) & (place >= starts), 1.0, 0.0).astype(BF16)


def in_hbm(*arrays):
    return [pltpu.with_memory_space_constraint(a, pltpu.HBM) for a in arrays]


def project_kernel(
    other_ref, lengths_hbm, owner_hbm, gain_hbm, x_hbm, wq_hbm, wk_hbm, wv_hbm,
    q_ref, k_ref, v_ref, rows_ref, columns_ref, slot_ref,
    lengths_ref, owner_ref, gain_ref, x_ref, wq_ref, wk_ref, wv_ref, sems, *, wide, capacity,
):
    sources = (lengths_hbm, owner_hbm, gain_hbm, x_hbm, wq_hbm, wk_hbm, wv_hbm)
    here = (lengths_ref, owner_ref, gain_ref, x_ref, wq_ref, wk_ref, wv_ref)
    copies = [pltpu.make_async_copy(s, d, sems.at[i]) for i, (s, d) in enumerate(zip(sources, here))]
    for copy in copies:
        copy.start()
    for copy in copies[:3]:
        copy.wait()
    packs, seq, width = x_ref.shape
    per_pack = lengths_ref.shape[1]
    for pack in range(packs):
        rows_ref[pack * seq : (pack + 1) * seq] = item_rows(lengths_ref[pack : pack + 1], seq)
        for side, ref in enumerate((lengths_ref, other_ref)):
            at = (side * packs + pack) * per_pack
            columns_ref[at : at + per_pack] = item_columns(ref[pack : pack + 1], seq)
    owner = owner_ref[...]
    items = owner.shape[1]
    target = jnp.where(lax.broadcasted_iota(jnp.int32, (wide, items), 0) == owner, 1.0, 0.0)
    before = lax.broadcasted_iota(jnp.int32, (items, items), 0) < lax.broadcasted_iota(jnp.int32, (items, items), 1)
    earlier = dot(target.astype(BF16), jnp.where(before, 1.0, 0.0).astype(BF16))
    rank = jnp.sum(earlier * target, axis=0, keepdims=True)
    slot_ref[...] = owner * capacity + rank.astype(jnp.int32)
    gain = gain_ref[...][None]
    copies[3].wait()
    normed = [rms(x_ref[pack].astype(F32), gain).astype(BF16) for pack in range(packs)]
    normed = jnp.concatenate(normed, axis=0)
    for copy, w_ref, out_ref in zip(copies[4:], (wq_ref, wk_ref, wv_ref), (q_ref, k_ref, v_ref)):
        copy.wait()
        out_ref[...] = dot(normed, w_ref[...]).astype(BF16)


def project(lengths, other, owner, x, gain, wq, wk, wv, wide, capacity):
    packs, seq, width = x.shape
    items = lengths.shape[1]
    sources = (lengths, owner, gain, x, wq, wk, wv)
    return pl.pallas_call(
        functools.partial(project_kernel, wide=wide, capacity=capacity),
        in_specs=[pl.BlockSpec(memory_space=pltpu.VMEM)] + [pl.BlockSpec(memory_space=pltpu.HBM)] * len(sources),
        out_shape=(
            jax.ShapeDtypeStruct((packs * seq, width), BF16),
            jax.ShapeDtypeStruct((packs * seq, width), BF16),
            jax.ShapeDtypeStruct((packs * seq, width), BF16),
            jax.ShapeDtypeStruct((packs * seq, items), BF16),
            jax.ShapeDtypeStruct((2 * packs * items, seq), BF16),
            jax.ShapeDtypeStruct(owner.shape, jnp.int32),
        ),
        scratch_shapes=[pltpu.VMEM(a.shape, a.dtype) for a in sources]
        + [pltpu.SemaphoreType.DMA((len(sources),))],
        compiler_params=params(),
        cost_estimate=cost(),
        name="project",
    )(other, *in_hbm(*sources))


def hold_kernel(common, group_ref, w_in_hbm, w_down_hbm, held_ref, sems):
    half = (w_in_hbm.shape[0] - common) // 2
    start = pl.multiple_of(common + group_ref[0, 0] * half, 16)
    copies, at = [], 0
    for first, size in ((0, common), (start, half)):
        for source in (w_in_hbm, w_down_hbm):
            copies.append(
                pltpu.make_async_copy(source.at[pl.ds(first, size)], held_ref.at[pl.ds(at, size)], sems.at[len(copies)])
            )
            at += size
    for copy in copies:
        copy.start()
    for copy in copies:
        copy.wait()


def hold(w_input, w_down, common):
    rows, width = w_input.shape
    far = pl.BlockSpec(memory_space=pltpu.HBM)
    return pl.pallas_call(
        functools.partial(hold_kernel, common),
        in_specs=[pl.BlockSpec(memory_space=pltpu.SMEM), far, far],
        out_shape=jax.ShapeDtypeStruct((rows + common, width), BF16),
        scratch_shapes=[pltpu.SemaphoreType.DMA((4,))],
        compiler_params=params(),
        cost_estimate=cost(),
        name="hold",
    )(lax.axis_index("groups").astype(jnp.int32).reshape(1, 1), *in_hbm(w_input, w_down))


def attend_kernel(
    pack, q_ref, k_ref, v_ref, rows_ref, columns_ref, x_ref, wo_ref, gain_ref,
    normed2_ref, pooled_ref, ctx_ref,
):
    _, seq, width = x_ref.shape
    items = rows_ref.shape[1]
    head = width // HEADS
    base = pack * seq
    onehot = rows_ref[base : base + seq]
    block, window, lanes = 64, 128, 256
    heads = lanes // head
    lane_head = lax.broadcasted_iota(jnp.int32, (block, lanes), 1) // head
    for start in range(0, seq, block):
        first = min(max(start - (window - block) // 2, 0), seq - window)
        same = dot_nt(onehot[start : start + block], onehot[first : first + window])
        same = jnp.concatenate([same] * heads, axis=0) > 0.5
        keys = slice(base + first, base + first + window)
        for column in range(0, width, lanes):
            across = slice(column, column + lanes)
            query = q_ref[base + start : base + start + block, across]
            stacked = jnp.concatenate(
                [jnp.where(lane_head == h, query, jnp.zeros_like(query)) for h in range(heads)], axis=0
            )
            scores = jnp.where(same, dot_nt(stacked, k_ref[keys, across]), -1e30)
            expo = jnp.exp(scores - jnp.max(scores, axis=-1, keepdims=True))
            probs = (expo * (1.0 / jnp.sum(expo, axis=-1, keepdims=True))).astype(BF16)
            mixed = dot(probs, v_ref[keys, across])
            context = mixed[:block]
            for h in range(1, heads):
                context = jnp.where(lane_head == h, mixed[h * block : (h + 1) * block], context)
            ctx_ref[start : start + block, across] = context.astype(BF16)
    stream = (x_ref[pack].astype(F32) + dot(ctx_ref[...], wo_ref[...])).astype(BF16)
    normed2_ref[...] = rms(stream.astype(F32), gain_ref[...][None]).astype(BF16)
    pooled_ref[...] = dot(columns_ref[pack * items : (pack + 1) * items], stream)


def attend(pack, projected, x, wo, gain2):
    _, seq, width = x.shape
    items = projected[3].shape[1]
    return pl.pallas_call(
        functools.partial(attend_kernel, pack),
        out_shape=(
            jax.ShapeDtypeStruct((seq, width), BF16),
            jax.ShapeDtypeStruct((items, width), F32),
        ),
        scratch_shapes=[pltpu.VMEM((seq, width), BF16)],
        compiler_params=params(),
        cost_estimate=cost(),
        name="attend",
    )(*projected[:5], x, wo, gain2)


def feed_side_kernel(side, n_held, pieces, columns_ref, *refs):
    normed_refs, held, (base_ref, out_ref) = refs[: -2 - n_held], refs[-2 - n_held : -2], refs[-2:]
    w_in = jnp.concatenate([held[i][r] for i, r, _, _ in pieces], axis=0)
    w_down = jnp.concatenate([held[i][r] for _, _, i, r in pieces], axis=0)
    packs = len(normed_refs)
    items = columns_ref.shape[0] // (2 * packs)
    pooled = []
    for pack in range(packs):
        hidden = jnp.maximum(dot_nt(normed_refs[pack][...], w_in), 0.0).astype(BF16)
        at = (side * packs + pack) * items
        pooled.append(dot(columns_ref[at : at + items], hidden).astype(BF16))
    out_ref[...] = base_ref[...] + dot(jnp.concatenate(pooled, axis=0), w_down)


def feed_side(side, columns, normed, held, pieces, base):
    return pl.pallas_call(
        functools.partial(feed_side_kernel, side, len(held), pieces),
        out_shape=jax.ShapeDtypeStruct(base.shape, F32),
        compiler_params=params(),
        cost_estimate=cost(),
        name="feed_side",
    )(columns, *normed[side], *held, base)


def feed_kernel(n_normed, n_held, pieces, n_base, columns_ref, *refs):
    normed_refs, refs = (refs[:n_normed], refs[n_normed : 2 * n_normed]), refs[2 * n_normed :]
    held, refs = refs[:n_held], refs[n_held:]
    bases, outs = (refs[: n_base[0]], refs[n_base[0] : sum(n_base)]), refs[sum(n_base) :]
    w_in = jnp.concatenate([held[i][r] for i, r, _, _ in pieces], axis=0)
    w_down = jnp.concatenate([held[i][r] for _, _, i, r in pieces], axis=0)
    packs = n_normed
    items = columns_ref.shape[0] // (2 * packs)
    for side in range(2):
        pooled = []
        for pack in range(packs):
            hidden = jnp.maximum(dot_nt(normed_refs[side][pack][...], w_in), 0.0).astype(BF16)
            at = (side * packs + pack) * items
            pooled.append(dot(columns_ref[at : at + items], hidden).astype(BF16))
        part = dot(jnp.concatenate(pooled, axis=0), w_down)
        if bases[side]:
            part = part + jnp.concatenate([r[...] for r in bases[side]], axis=0)
        outs[side][...] = part


def feed(columns, normed, held, pieces, bases):
    items = columns.shape[0] // 2
    width = held[0].shape[1]
    n_base = tuple(len(b) for b in bases)
    return pl.pallas_call(
        functools.partial(feed_kernel, len(normed[0]), len(held), pieces, n_base),
        out_shape=(jax.ShapeDtypeStruct((items, width), F32),) * 2,
        compiler_params=params(),
        cost_estimate=cost(),
        name="feed",
    )(columns, *normed[0], *normed[1], *held, *bases[0], *bases[1])


def place_kernel(acc_ref, other_ref, gain_ref, slot_ref, cluster_ref, embed_ref, send_ref):
    width = embed_ref.shape[1]
    embed = rms(acc_ref[...] + other_ref[...], gain_ref[...][None]).astype(BF16)
    embed_ref[...] = embed
    slots, items = send_ref.shape[0], embed.shape[0]
    placing = jnp.where(
        lax.broadcasted_iota(jnp.int32, (slots, items), 0) == slot_ref[...], 1.0, 0.0
    ).astype(BF16)
    send_ref[:, :width] = dot(placing, embed).astype(BF16)
    clusters = send_ref.shape[1] - width
    chosen = jnp.where(
        lax.broadcasted_iota(jnp.int32, (clusters, items), 0) == cluster_ref[...], 1.0, 0.0
    ).astype(BF16)
    send_ref[:, width:] = dot_nt(placing, chosen).astype(BF16)


def code_kernel(rows_ref, coarse_ref, books_ref, out_ref):
    clusters, codes, width = books_ref.shape
    slots = rows_ref.shape[0]
    spare = -clusters % 16
    coarse = jnp.concatenate([coarse_ref[...], jnp.zeros((spare, width), BF16)], axis=0)
    rows = jnp.concatenate([rows_ref[:, :width], coarse], axis=0)
    total = jnp.zeros((slots, codes), F32)
    for cluster in range(clusters):
        direct = dot_nt(rows, books_ref[cluster])
        offset = direct[slots + cluster : slots + cluster + 1]
        chosen = rows_ref[:, width + cluster : width + cluster + 1].astype(F32)
        total = total + (direct[:slots] - offset) * chosen
    out_ref[...] = total.astype(BF16)


def take_kernel(slot_ref, codes_ref, out_ref):
    slots, items = codes_ref.shape[0], slot_ref.shape[1]
    placing = jnp.where(
        lax.broadcasted_iota(jnp.int32, (slots, items), 0) == slot_ref[...], 1.0, 0.0
    ).astype(BF16)
    out_ref[...] = lax.dot_general(
        placing, codes_ref[...], (((0,), (0,)), ((), ())), preferred_element_type=F32
    )


def flip(axis_name, count, bits):
    pairs = [(i, i ^ bits) for i in range(count)]
    return lambda value: lax.ppermute(value, axis_name, pairs)


def gather_any(w_input, w_down, count):
    groups = [list(range(core, count, 2)) for core in range(2)]
    w_in = lax.all_gather(w_input, "wide", axis=0, tiled=True, axis_index_groups=groups)
    down = lax.all_gather(w_down, "wide", axis=0, tiled=True, axis_index_groups=groups)
    return w_in, down


def overlapped(w_input, w_down, tokens, encode_first, encode, sibling):
    rows = w_input.shape[0]
    common = rows // 3 // 16 * 16
    half = (rows - common) // 2
    split, both, every = 2 * common, 2 * half, 2 * (common + half)
    near, side, twin = flip("wide", 16, 4), flip("wide", 16, 2), flip("groups", 2, 1)
    line = lax.axis_index("wide") // 4
    inner = (line == 1) | (line == 2)

    def along(value, hops):
        pairs = [(4 * a + i, 4 * b + i) for a, b in hops for i in range(4)]
        return lax.ppermute(value, "wide", pairs)

    def amid(value):
        pairs = [(i, i ^ 12 if i // 4 in (1, 2) else i ^ 1) for i in range(16)]
        return lax.ppermute(value, "wide", pairs)

    after = lax.optimization_barrier

    def blocks(i):
        return [
            (i, slice(0, common), i, slice(common, split)),
            (i, slice(split, split + half), i, slice(split + half, every)),
        ]

    def rest(i, at=0):
        return [(i, slice(at, at + half), i, slice(at + half, at + both))]

    def cat(a, b):
        return jnp.concatenate([a, b], axis=0)

    held = hold(w_input, w_down, common)
    middle, near1, side0 = amid(held), near(held), side(held)
    projected = encode_first(tokens)
    side0, near1, middle, projected = after((side0, near1, middle, projected))
    columns = projected[4]

    far2 = along(jnp.where(inner, middle, held), [(1, 0), (0, 2), (2, 3), (3, 1)])
    x0 = twin(cat(side0[split:], near1[split:]))
    side1 = side(near1)
    first = encode(0, projected, tokens)
    side1, far2, first, projected = after((side1, far2, first, projected))

    side2, outer = side(far2), near(far2)
    x0, projected = after((x0, projected))
    x1 = twin(cat(side1[split:], far2[split:]))
    last_inner = amid(x0[:both])
    second = encode(1, projected, tokens)
    side2, x1, outer, last_inner, second = after((side2, x1, outer, last_inner, second))

    far3 = jnp.where(inner, middle, outer)
    side3, x2 = side(far3), twin(cat(side2[split:], far3[split:]))
    last_outer = along(x1[:both], [(2, 0), (0, 1), (1, 3), (3, 2)])
    normed = ((first[0], second[0]), (sibling(first[0]), sibling(second[0])))
    own = [(0, slice(0, rows), 1, slice(0, rows))]
    pieces = own + blocks(2) + rest(3) + blocks(4) + rest(3, both) + blocks(5) + rest(6)
    acc = feed(columns, normed, [w_input, w_down, side0, x0, near1, side1, x1], pieces, ([first[1], second[1]], []))
    pieces = blocks(0) + rest(1, both) + blocks(2) + blocks(3)
    acc = feed(columns, normed, [far2, x1, side2, far3], pieces, ([acc[0]], [acc[1]]))
    side3, x2, last_outer, acc = after((side3, x2, last_outer, acc))

    last = jnp.where(inner, last_inner, last_outer)
    pieces = rest(0) + rest(0, both) + blocks(1) + rest(2)
    held = [x2, side3, last]
    there = sibling(feed_side(1, columns, normed, held, pieces, acc[1]))
    return feed_side(0, columns, normed, held, pieces, acc[0]), there, projected[5]


def local(
    tokens, item_lengths, w_query, w_key, w_value, w_output, w_input, w_down,
    norm_attn, norm_ffn, norm_final, owner, cluster_slot, coarse, centroids,
):
    packs, seq, width = tokens.shape
    per_pack = item_lengths.shape[1]
    wide_count = lax.axis_size("wide")
    items_dev = packs * per_pack
    capacity = max(2, 2 * items_dev // wide_count)
    slots = wide_count * capacity
    local_clusters, codes_count, _ = centroids.shape
    sibling = flip("wide", wide_count, 1)

    other_lengths = sibling(item_lengths)

    def encode_first(tokens):
        return project(
            item_lengths, other_lengths, owner.reshape(1, items_dev), tokens, norm_attn,
            w_query, w_key, w_value, wide_count, capacity,
        )

    def encode(pack, projected, tokens):
        return attend(pack, projected, tokens, w_output, norm_ffn)

    if wide_count == 16 and packs == 2:
        acc, other, slots_of = overlapped(w_input, w_down, tokens, encode_first, encode, sibling)
    else:
        projected = encode_first(tokens)
        slots_of = projected[5]
        normed, pooled = zip(*[encode(p, projected, tokens) for p in range(packs)])
        held = gather_any(w_input, w_down, wide_count)
        every = slice(0, held[0].shape[0])
        normed = (normed, [sibling(n) for n in normed])
        acc = feed(projected[4], normed, held, [(0, every, 1, every)], (pooled, []))
        acc, other = acc[0], sibling(acc[1])

    item_embed, send = pl.pallas_call(
        place_kernel,
        out_shape=(
            jax.ShapeDtypeStruct((items_dev, width), BF16),
            jax.ShapeDtypeStruct((slots, width + 128), BF16),
        ),
        compiler_params=params(),
        name="place",
    )(acc, other, norm_final, slots_of, cluster_slot[None])
    send = send.reshape(wide_count, capacity, width + 128)
    rows = lax.all_to_all(send, "wide", split_axis=0, concat_axis=0, tiled=True)
    codes = pl.pallas_call(
        code_kernel,
        out_shape=jax.ShapeDtypeStruct((slots, codes_count), BF16),
        compiler_params=params(),
        name="codes",
    )(rows.reshape(slots, width + 128), coarse, centroids)
    codes = codes.reshape(wide_count, capacity, codes_count)
    returned = lax.all_to_all(codes, "wide", split_axis=0, concat_axis=0, tiled=True)
    item_codes = pl.pallas_call(
        take_kernel,
        out_shape=jax.ShapeDtypeStruct((items_dev, codes_count), F32),
        compiler_params=params(),
        cost_estimate=cost(),
        name="take",
    )(slots_of, returned.reshape(slots, codes_count))
    return (item_embed, item_codes)


def solution(mesh):
    return jax.shard_map(
        local,
        mesh=mesh,
        in_specs=(
            P(("groups", "wide"), None, None),
            P(("groups", "wide"), None),
            P(),
            P(),
            P(),
            P(),
            P("wide", None),
            P("wide", None),
            P(),
            P(),
            P(),
            P(("groups", "wide"), None),
            P(("groups", "wide")),
            P("wide", None),
            P("wide", None, None),
        ),
        out_specs=(P(("groups", "wide"), None), P(("groups", "wide"), None)),
        check_vma=False,
    )
```

```python
import functools

import jax
import jax.numpy as jnp
from jax import lax
from jax.experimental import pallas as pl
from jax.experimental.pallas import tpu as pltpu
from jax.sharding import PartitionSpec as P

HEADS = 12
EPS = 1e-06
VMEM_BYTES = 16 * 1024 * 1024
F32 = jnp.float32
BF16 = jnp.bfloat16


def params():
    return pltpu.CompilerParams(vmem_limit_bytes=VMEM_BYTES)


def cost():
    return pl.CostEstimate(flops=2000000000, bytes_accessed=5000000, transcendentals=0)


def dot(a, b):
    return jnp.dot(a, b, preferred_element_type=F32)


def dot_nt(a, b):
    return lax.dot_general(a, b, (((1,), (1,)), ((), ())), preferred_element_type=F32)


def rms(values, gain):
    mean_sq = jnp.mean(values * values, axis=-1, keepdims=True)
    return values * lax.rsqrt(mean_sq + EPS) * gain


def item_rows(lengths, seq):
    items = lengths.shape[1]
    tri = (
        lax.broadcasted_iota(jnp.int32, (items, items), 0)
        <= lax.broadcasted_iota(jnp.int32, (items, items), 1)
    ).astype(F32)
    rows = jnp.broadcast_to(lengths.astype(F32), (8, items))
    ends = dot(rows.astype(BF16), tri.astype(BF16))[:1]
    starts = ends - rows[:1]
    place = lax.broadcasted_iota(jnp.int32, (seq, items), 0).astype(F32)
    return jnp.where((place < ends) & (place >= starts), 1.0, 0.0).astype(BF16)


def item_columns(lengths, seq):
    items = lengths.shape[1]
    row = lax.broadcasted_iota(jnp.int32, (items, items), 0)
    column = lax.broadcasted_iota(jnp.int32, (items, items), 1)
    rows = jnp.broadcast_to(lengths.astype(F32), (8, items)).astype(BF16)
    ends = dot_nt((column <= row).astype(F32).astype(BF16), rows)[:, :1]
    starts = dot_nt((column < row).astype(F32).astype(BF16), rows)[:, :1]
    place = lax.broadcasted_iota(jnp.int32, (items, seq), 1).astype(F32)
    return jnp.where((place < ends) & (place >= starts), 1.0, 0.0).astype(BF16)


def in_hbm(*arrays):
    return [pltpu.with_memory_space_constraint(a, pltpu.HBM) for a in arrays]


def project_kernel(
    other_ref, lengths_hbm, owner_hbm, gain_hbm, x_hbm, wq_hbm, wk_hbm, wv_hbm,
    q_ref, k_ref, v_ref, rows_ref, columns_ref, slot_ref,
    lengths_ref, owner_ref, gain_ref, x_ref, wq_ref, wk_ref, wv_ref, sems, *, wide, capacity,
):
    sources = (lengths_hbm, owner_hbm, gain_hbm, x_hbm, wq_hbm, wk_hbm, wv_hbm)
    here = (lengths_ref, owner_ref, gain_ref, x_ref, wq_ref, wk_ref, wv_ref)
    copies = [pltpu.make_async_copy(s, d, sems.at[i]) for i, (s, d) in enumerate(zip(sources, here))]
    for copy in copies:
        copy.start()
    for copy in copies[:3]:
        copy.wait()
    packs, seq, width = x_ref.shape
    per_pack = lengths_ref.shape[1]
    for pack in range(packs):
        rows_ref[pack * seq : (pack + 1) * seq] = item_rows(lengths_ref[pack : pack + 1], seq)
        for side, ref in enumerate((lengths_ref, other_ref)):
            at = (side * packs + pack) * per_pack
            columns_ref[at : at + per_pack] = item_columns(ref[pack : pack + 1], seq)
    owner = owner_ref[...]
    items = owner.shape[1]
    target = jnp.where(lax.broadcasted_iota(jnp.int32, (wide, items), 0) == owner, 1.0, 0.0)
    before = lax.broadcasted_iota(jnp.int32, (items, items), 0) < lax.broadcasted_iota(jnp.int32, (items, items), 1)
    earlier = dot(target.astype(BF16), jnp.where(before, 1.0, 0.0).astype(BF16))
    rank = jnp.sum(earlier * target, axis=0, keepdims=True)
    slot_ref[...] = owner * capacity + rank.astype(jnp.int32)
    gain = gain_ref[...][None]
    copies[3].wait()
    normed = [rms(x_ref[pack].astype(F32), gain).astype(BF16) for pack in range(packs)]
    normed = jnp.concatenate(normed, axis=0)
    for copy, w_ref, out_ref in zip(copies[4:], (wq_ref, wk_ref, wv_ref), (q_ref, k_ref, v_ref)):
        copy.wait()
        out_ref[...] = dot(normed, w_ref[...]).astype(BF16)


def project(lengths, other, owner, x, gain, wq, wk, wv, wide, capacity):
    packs, seq, width = x.shape
    items = lengths.shape[1]
    sources = (lengths, owner, gain, x, wq, wk, wv)
    return pl.pallas_call(
        functools.partial(project_kernel, wide=wide, capacity=capacity),
        in_specs=[pl.BlockSpec(memory_space=pltpu.VMEM)] + [pl.BlockSpec(memory_space=pltpu.HBM)] * len(sources),
        out_shape=(
            jax.ShapeDtypeStruct((packs * seq, width), BF16),
            jax.ShapeDtypeStruct((packs * seq, width), BF16),
            jax.ShapeDtypeStruct((packs * seq, width), BF16),
            jax.ShapeDtypeStruct((packs * seq, items), BF16),
            jax.ShapeDtypeStruct((2 * packs * items, seq), BF16),
            jax.ShapeDtypeStruct(owner.shape, jnp.int32),
        ),
        scratch_shapes=[pltpu.VMEM(a.shape, a.dtype) for a in sources]
        + [pltpu.SemaphoreType.DMA((len(sources),))],
        compiler_params=params(),
        cost_estimate=cost(),
        name="project",
    )(other, *in_hbm(*sources))


def hold_kernel(common, group_ref, w_in_hbm, w_down_hbm, held_ref, sems):
    half = (w_in_hbm.shape[0] - common) // 2
    start = pl.multiple_of(common + group_ref[0, 0] * half, 16)
    copies, at = [], 0
    for first, size in ((0, common), (start, half)):
        for source in (w_in_hbm, w_down_hbm):
            copies.append(
                pltpu.make_async_copy(source.at[pl.ds(first, size)], held_ref.at[pl.ds(at, size)], sems.at[len(copies)])
            )
            at += size
    for copy in copies:
        copy.start()
    for copy in copies:
        copy.wait()


def hold(w_input, w_down, common):
    rows, width = w_input.shape
    far = pl.BlockSpec(memory_space=pltpu.HBM)
    return pl.pallas_call(
        functools.partial(hold_kernel, common),
        in_specs=[pl.BlockSpec(memory_space=pltpu.SMEM), far, far],
        out_shape=jax.ShapeDtypeStruct((rows + common, width), BF16),
        scratch_shapes=[pltpu.SemaphoreType.DMA((4,))],
        compiler_params=params(),
        cost_estimate=cost(),
        name="hold",
    )(lax.axis_index("groups").astype(jnp.int32).reshape(1, 1), *in_hbm(w_input, w_down))


def attend_kernel(
    pack, q_ref, k_ref, v_ref, rows_ref, columns_ref, x_ref, wo_ref, gain_ref,
    normed2_ref, pooled_ref, ctx_ref,
):
    _, seq, width = x_ref.shape
    items = rows_ref.shape[1]
    head = width // HEADS
    base = pack * seq
    onehot = rows_ref[base : base + seq]
    block, window, lanes = 64, 128, 256
    heads = lanes // head
    lane_head = lax.broadcasted_iota(jnp.int32, (block, lanes), 1) // head
    for start in range(0, seq, block):
        first = min(max(start - (window - block) // 2, 0), seq - window)
        same = dot_nt(onehot[start : start + block], onehot[first : first + window])
        same = jnp.concatenate([same] * heads, axis=0) > 0.5
        keys = slice(base + first, base + first + window)
        for column in range(0, width, lanes):
            across = slice(column, column + lanes)
            query = q_ref[base + start : base + start + block, across]
            stacked = jnp.concatenate(
                [jnp.where(lane_head == h, query, jnp.zeros_like(query)) for h in range(heads)], axis=0
            )
            scores = jnp.where(same, dot_nt(stacked, k_ref[keys, across]), -1e30)
            expo = jnp.exp(scores - jnp.max(scores, axis=-1, keepdims=True))
            probs = (expo * (1.0 / jnp.sum(expo, axis=-1, keepdims=True))).astype(BF16)
            mixed = dot(probs, v_ref[keys, across])
            context = mixed[:block]
            for h in range(1, heads):
                context = jnp.where(lane_head == h, mixed[h * block : (h + 1) * block], context)
            ctx_ref[start : start + block, across] = context.astype(BF16)
    stream = (x_ref[pack].astype(F32) + dot(ctx_ref[...], wo_ref[...])).astype(BF16)
    normed2_ref[...] = rms(stream.astype(F32), gain_ref[...][None]).astype(BF16)
    pooled_ref[...] = dot(columns_ref[pack * items : (pack + 1) * items], stream)


def attend(pack, projected, x, wo, gain2):
    _, seq, width = x.shape
    items = projected[3].shape[1]
    return pl.pallas_call(
        functools.partial(attend_kernel, pack),
        out_shape=(
            jax.ShapeDtypeStruct((seq, width), BF16),
            jax.ShapeDtypeStruct((items, width), F32),
        ),
        scratch_shapes=[pltpu.VMEM((seq, width), BF16)],
        compiler_params=params(),
        cost_estimate=cost(),
        name="attend",
    )(*projected[:5], x, wo, gain2)


def feed_side_kernel(side, n_held, pieces, columns_ref, *refs):
    normed_refs, held, (base_ref, out_ref) = refs[: -2 - n_held], refs[-2 - n_held : -2], refs[-2:]
    w_in = jnp.concatenate([held[i][r] for i, r, _, _ in pieces], axis=0)
    w_down = jnp.concatenate([held[i][r] for _, _, i, r in pieces], axis=0)
    packs = len(normed_refs)
    items = columns_ref.shape[0] // (2 * packs)
    pooled = []
    for pack in range(packs):
        hidden = jnp.maximum(dot_nt(normed_refs[pack][...], w_in), 0.0).astype(BF16)
        at = (side * packs + pack) * items
        pooled.append(dot(columns_ref[at : at + items], hidden).astype(BF16))
    out_ref[...] = base_ref[...] + dot(jnp.concatenate(pooled, axis=0), w_down)


def feed_side(side, columns, normed, held, pieces, base):
    return pl.pallas_call(
        functools.partial(feed_side_kernel, side, len(held), pieces),
        out_shape=jax.ShapeDtypeStruct(base.shape, F32),
        compiler_params=params(),
        cost_estimate=cost(),
        name="feed_side",
    )(columns, *normed[side], *held, base)


def feed_kernel(n_normed, n_held, pieces, n_base, columns_ref, *refs):
    normed_refs, refs = (refs[:n_normed], refs[n_normed : 2 * n_normed]), refs[2 * n_normed :]
    held, refs = refs[:n_held], refs[n_held:]
    bases, outs = (refs[: n_base[0]], refs[n_base[0] : sum(n_base)]), refs[sum(n_base) :]
    w_in = jnp.concatenate([held[i][r] for i, r, _, _ in pieces], axis=0)
    w_down = jnp.concatenate([held[i][r] for _, _, i, r in pieces], axis=0)
    packs = n_normed
    items = columns_ref.shape[0] // (2 * packs)
    for side in range(2):
        pooled = []
        for pack in range(packs):
            hidden = jnp.maximum(dot_nt(normed_refs[side][pack][...], w_in), 0.0).astype(BF16)
            at = (side * packs + pack) * items
            pooled.append(dot(columns_ref[at : at + items], hidden).astype(BF16))
        part = dot(jnp.concatenate(pooled, axis=0), w_down)
        if bases[side]:
            part = part + jnp.concatenate([r[...] for r in bases[side]], axis=0)
        outs[side][...] = part


def feed(columns, normed, held, pieces, bases):
    items = columns.shape[0] // 2
    width = held[0].shape[1]
    n_base = tuple(len(b) for b in bases)
    return pl.pallas_call(
        functools.partial(feed_kernel, len(normed[0]), len(held), pieces, n_base),
        out_shape=(jax.ShapeDtypeStruct((items, width), F32),) * 2,
        compiler_params=params(),
        cost_estimate=cost(),
        name="feed",
    )(columns, *normed[0], *normed[1], *held, *bases[0], *bases[1])


def place_kernel(acc_ref, other_ref, gain_ref, slot_ref, cluster_ref, embed_ref, send_ref):
    width = embed_ref.shape[1]
    embed = rms(acc_ref[...] + other_ref[...], gain_ref[...][None]).astype(BF16)
    embed_ref[...] = embed
    slots, items = send_ref.shape[0], embed.shape[0]
    placing = jnp.where(
        lax.broadcasted_iota(jnp.int32, (slots, items), 0) == slot_ref[...], 1.0, 0.0
    ).astype(BF16)
    send_ref[:, :width] = dot(placing, embed).astype(BF16)
    clusters = send_ref.shape[1] - width
    chosen = jnp.where(
        lax.broadcasted_iota(jnp.int32, (clusters, items), 0) == cluster_ref[...], 1.0, 0.0
    ).astype(BF16)
    send_ref[:, width:] = dot_nt(placing, chosen).astype(BF16)


def code_kernel(rows_ref, coarse_ref, books_ref, out_ref):
    clusters, codes, width = books_ref.shape
    slots = rows_ref.shape[0]
    spare = -clusters % 16
    coarse = jnp.concatenate([coarse_ref[...], jnp.zeros((spare, width), BF16)], axis=0)
    rows = jnp.concatenate([rows_ref[:, :width], coarse], axis=0)
    total = jnp.zeros((slots, codes), F32)
    for cluster in range(clusters):
        direct = dot_nt(rows, books_ref[cluster])
        offset = direct[slots + cluster : slots + cluster + 1]
        chosen = rows_ref[:, width + cluster : width + cluster + 1].astype(F32)
        total = total + (direct[:slots] - offset) * chosen
    out_ref[...] = total.astype(BF16)


def take_kernel(slot_ref, codes_ref, out_ref):
    slots, items = codes_ref.shape[0], slot_ref.shape[1]
    placing = jnp.where(
        lax.broadcasted_iota(jnp.int32, (slots, items), 0) == slot_ref[...], 1.0, 0.0
    ).astype(BF16)
    out_ref[...] = lax.dot_general(
        placing, codes_ref[...], (((0,), (0,)), ((), ())), preferred_element_type=F32
    )


def flip(axis_name, count, bits):
    pairs = [(i, i ^ bits) for i in range(count)]
    return lambda value: lax.ppermute(value, axis_name, pairs)


def gather_any(w_input, w_down, count):
    groups = [list(range(core, count, 2)) for core in range(2)]
    w_in = lax.all_gather(w_input, "wide", axis=0, tiled=True, axis_index_groups=groups)
    down = lax.all_gather(w_down, "wide", axis=0, tiled=True, axis_index_groups=groups)
    return w_in, down


def overlapped(w_input, w_down, tokens, encode_first, encode, sibling):
    rows = w_input.shape[0]
    common = rows // 3 // 16 * 16
    half = (rows - common) // 2
    split, both, every = 2 * common, 2 * half, 2 * (common + half)
    near, side, twin = flip("wide", 16, 4), flip("wide", 16, 2), flip("groups", 2, 1)
    line = lax.axis_index("wide") // 4
    inner = (line == 1) | (line == 2)

    def along(value, hops):
        pairs = [(4 * a + i, 4 * b + i) for a, b in hops for i in range(4)]
        return lax.ppermute(value, "wide", pairs)

    def amid(value):
        pairs = [(i, i ^ 12 if i // 4 in (1, 2) else i ^ 1) for i in range(16)]
        return lax.ppermute(value, "wide", pairs)

    after = lax.optimization_barrier

    def blocks(i):
        return [
            (i, slice(0, common), i, slice(common, split)),
            (i, slice(split, split + half), i, slice(split + half, every)),
        ]

    def rest(i, at=0):
        return [(i, slice(at, at + half), i, slice(at + half, at + both))]

    def cat(a, b):
        return jnp.concatenate([a, b], axis=0)

    held = hold(w_input, w_down, common)
    middle, near1, side0 = amid(held), near(held), side(held)
    projected = encode_first(tokens)
    side0, near1, middle, projected = after((side0, near1, middle, projected))
    columns = projected[4]

    far2 = along(jnp.where(inner, middle, held), [(1, 0), (0, 2), (2, 3), (3, 1)])
    x0 = twin(cat(side0[split:], near1[split:]))
    side1 = side(near1)
    first = encode(0, projected, tokens)
    side1, far2, first, projected = after((side1, far2, first, projected))

    side2, outer = side(far2), near(far2)
    x0, projected = after((x0, projected))
    x1 = twin(cat(side1[split:], far2[split:]))
    last_inner = amid(x0[:both])
    second = encode(1, projected, tokens)
    side2, x1, outer, last_inner, second = after((side2, x1, outer, last_inner, second))

    far3 = jnp.where(inner, middle, outer)
    x2, side3 = twin(cat(side2[split:], far3[split:])), side(far3)
    last_outer = along(x1[:both], [(2, 0), (0, 1), (1, 3), (3, 2)])
    normed = ((first[0], second[0]), (sibling(first[0]), sibling(second[0])))
    own = [(0, slice(0, rows), 1, slice(0, rows))]
    pieces = own + blocks(2) + rest(3) + blocks(4) + rest(3, both) + blocks(5) + rest(6)
    acc = feed(columns, normed, [w_input, w_down, side0, x0, near1, side1, x1], pieces, ([first[1], second[1]], []))
    pieces = blocks(0) + rest(1, both) + blocks(2) + blocks(3)
    acc = feed(columns, normed, [far2, x1, side2, far3], pieces, ([acc[0]], [acc[1]]))
    side3, x2, last_outer, acc = after((side3, x2, last_outer, acc))

    last = jnp.where(inner, last_inner, last_outer)
    pieces = rest(0) + rest(0, both) + blocks(1) + rest(2)
    held = [x2, side3, last]
    there = sibling(feed_side(1, columns, normed, held, pieces, acc[1]))
    return feed_side(0, columns, normed, held, pieces, acc[0]), there, projected[5]


def local(
    tokens, item_lengths, w_query, w_key, w_value, w_output, w_input, w_down,
    norm_attn, norm_ffn, norm_final, owner, cluster_slot, coarse, centroids,
):
    packs, seq, width = tokens.shape
    per_pack = item_lengths.shape[1]
    wide_count = lax.axis_size("wide")
    items_dev = packs * per_pack
    capacity = max(2, 2 * items_dev // wide_count)
    slots = wide_count * capacity
    local_clusters, codes_count, _ = centroids.shape
    sibling = flip("wide", wide_count, 1)

    other_lengths = sibling(item_lengths)

    def encode_first(tokens):
        return project(
            item_lengths, other_lengths, owner.reshape(1, items_dev), tokens, norm_attn,
            w_query, w_key, w_value, wide_count, capacity,
        )

    def encode(pack, projected, tokens):
        return attend(pack, projected, tokens, w_output, norm_ffn)

    if wide_count == 16 and packs == 2:
        acc, other, slots_of = overlapped(w_input, w_down, tokens, encode_first, encode, sibling)
    else:
        projected = encode_first(tokens)
        slots_of = projected[5]
        normed, pooled = zip(*[encode(p, projected, tokens) for p in range(packs)])
        held = gather_any(w_input, w_down, wide_count)
        every = slice(0, held[0].shape[0])
        normed = (normed, [sibling(n) for n in normed])
        acc = feed(projected[4], normed, held, [(0, every, 1, every)], (pooled, []))
        acc, other = acc[0], sibling(acc[1])

    item_embed, send = pl.pallas_call(
        place_kernel,
        out_shape=(
            jax.ShapeDtypeStruct((items_dev, width), BF16),
            jax.ShapeDtypeStruct((slots, width + 128), BF16),
        ),
        compiler_params=params(),
        name="place",
    )(acc, other, norm_final, slots_of, cluster_slot[None])
    send = send.reshape(wide_count, capacity, width + 128)
    rows = lax.all_to_all(send, "wide", split_axis=0, concat_axis=0, tiled=True)
    codes = pl.pallas_call(
        code_kernel,
        out_shape=jax.ShapeDtypeStruct((slots, codes_count), BF16),
        compiler_params=params(),
        name="codes",
    )(rows.reshape(slots, width + 128), coarse, centroids)
    codes = codes.reshape(wide_count, capacity, codes_count)
    returned = lax.all_to_all(codes, "wide", split_axis=0, concat_axis=0, tiled=True)
    item_codes = pl.pallas_call(
        take_kernel,
        out_shape=jax.ShapeDtypeStruct((items_dev, codes_count), F32),
        compiler_params=params(),
        cost_estimate=cost(),
        name="take",
    )(slots_of, returned.reshape(slots, codes_count))
    return (item_embed, item_codes)


def solution(mesh):
    return jax.shard_map(
        local,
        mesh=mesh,
        in_specs=(
            P(("groups", "wide"), None, None),
            P(("groups", "wide"), None),
            P(),
            P(),
            P(),
            P(),
            P("wide", None),
            P("wide", None),
            P(),
            P(),
            P(),
            P(("groups", "wide"), None),
            P(("groups", "wide")),
            P("wide", None),
            P("wide", None, None),
        ),
        out_specs=(P(("groups", "wide"), None), P(("groups", "wide"), None)),
        check_vma=False,
    )
```
